32 devices in a mesh: ctx: 8 (over z, y), exp: 2 (over x), dp: 2 (over core).
Axes of the slice: x: 2, y: 2, z: 4, core: 2. Of those that a mesh axis runs over, the one named last changes fastest.
Arguments:
- hidden_in: bfloat16 [2, 2048, 1024], P('dp', ('ctx', 'exp')), may hold values from -6 to 6
- queries: bfloat16 [2, 2048, 1024], P('dp', ('ctx', 'exp')), may hold values from -6 to 6
- keys: bfloat16 [2, 2048, 1024], P('dp', ('ctx', 'exp')), may hold values from -6 to 6
- values: bfloat16 [2, 2048, 1024], P('dp', ('ctx', 'exp')), may hold values from -6 to 6
- log_decay: float32 [2, 2048, 8], P('dp', ('ctx', 'exp')), may hold values from -1 to 0
- retention_gain: float32 [1024], replicated, may hold values from 0.25 to 1.75
- norm_gain: float32 [1024], replicated, may hold values from 0.25 to 1.75
- routes: int32 [2, 2048, 2], P('dp', ('ctx', 'exp')), may hold values from 0 to 15, all different within a row; in each aligned block of 128 rows (0 to 127, 128 to 255, ..., all dimensions but the last counted through in order) at most 20 rows name the same one
- route_weights: float32 [2, 2048, 2], P('dp', ('ctx', 'exp')), may hold values from 0.1 to 1
- w_gate: bfloat16 [16, 1024, 1408], P(('ctx', 'dp'), 'exp'), may hold values from -0.1875 to 0.1875
- w_up: bfloat16 [16, 1024, 1408], P(('ctx', 'dp'), 'exp'), may hold values from -0.1875 to 0.1875
- w_down: bfloat16 [16, 1024, 1408], P(('ctx', 'dp'), 'exp'), may hold values from -0.15625 to 0.15625
Outputs:
- output: bfloat16 [2, 2048, 1024], P('dp', ('ctx', 'exp'))
The draws below stay inside these ranges and needn't reach their ends.
Inputs may be any that keep to these rules, and one draw needn't show every extreme that they name: `routes`: in each aligned block of 128 positions (the positions of one device) no expert is named more than 20 times, and a position's 2 experts differ.
All inputs are finite; a program needn't handle non-finite values.
Results may differ from the reference program's by a relative error of at most 0.007.
Values may be sent and summed in bfloat16 or wider, within the bound.
A program may use at most 128 MiB of HBM per device.

```python
import math
import jax
import jax.numpy as jnp
import numpy as np
from jax import lax

D = 1024
RETENTION_HEADS = 8
HK = 128
FF = 1408
TOP = 2
TOK_DEV = 128
EXPERTS = 16
CAP = 20
SEQUENCE_LENGTH = 2048
SEQUENCE_COUNT = 2


def draw_log_decay(key, part):
    random_subkeys = jax.random.split(key, 7)
    head_order = jax.random.permutation(random_subkeys[0], RETENTION_HEADS)
    quick_heads = jnp.broadcast_to((head_order < RETENTION_HEADS // 2)[None, None, :], (SEQUENCE_COUNT, 1, RETENTION_HEADS))
    slow_rate = jnp.exp(jax.random.uniform(random_subkeys[1], (SEQUENCE_COUNT, 1, RETENTION_HEADS), minval=math.log(0.05), maxval=math.log(0.3))) / SEQUENCE_LENGTH
    fast_rate = jnp.exp(jax.random.uniform(random_subkeys[2], (SEQUENCE_COUNT, 1, RETENTION_HEADS), minval=math.log(0.02), maxval=math.log(0.034)))
    decay_factor = jnp.where(quick_heads, fast_rate, slow_rate)
    block_decay_scale = jnp.exp(jax.random.uniform(random_subkeys[3], (SEQUENCE_COUNT, SEQUENCE_LENGTH // TOK_DEV, 1, RETENTION_HEADS), minval=math.log(0.5), maxval=math.log(2.0)))
    block_decay_scale = jnp.broadcast_to(block_decay_scale, (SEQUENCE_COUNT, SEQUENCE_LENGTH // TOK_DEV, TOK_DEV, RETENTION_HEADS)).reshape(SEQUENCE_COUNT, SEQUENCE_LENGTH, RETENTION_HEADS)
    step_decay_scale = jax.random.uniform(random_subkeys[4], (SEQUENCE_COUNT, SEQUENCE_LENGTH, RETENTION_HEADS), minval=0.5, maxval=1.5)
    spike_locations = jax.random.randint(random_subkeys[5], (SEQUENCE_COUNT, 2), 0, SEQUENCE_LENGTH)
    spike_penalty = jax.random.uniform(random_subkeys[6], (SEQUENCE_COUNT, 2, RETENTION_HEADS), minval=0.5, maxval=0.8)
    token_position = jnp.arange(SEQUENCE_LENGTH, dtype=jnp.int32)
    spike_events = jnp.zeros((SEQUENCE_COUNT, SEQUENCE_LENGTH, RETENTION_HEADS), jnp.float32)
    for spike_index in range(2):
        spike_mask = (spike_locations[:, spike_index][:, None] == token_position[None, :])[:, :, None]
        spike_events = spike_events + jnp.where(spike_mask, jnp.log(spike_penalty[:, spike_index, :])[:, None, :], 0.0)
    return (-decay_factor * block_decay_scale * step_decay_scale + spike_events).astype(jnp.float32)


def shard_levels(own_key, shape, pieces, smallest, top_value):
    factor_of = 1.0
    for dim, shards_of in pieces:
        steps = jax.random.uniform(jax.random.fold_in(jax.random.fold_in(own_key, 6), dim), (shards_of,), jnp.float32, smallest / len(pieces), top_value / len(pieces))
        factor_of = factor_of * jnp.repeat(jnp.exp(steps), shape[dim] // shards_of).reshape((-1,) + (1,) * (len(shape) - 1 - dim))
    return factor_of


def deal_out(rng, own, number, rows, count, top, limit, skew):
    order = jax.random.permutation(rng, count)
    packed, ordinary = portions_of(count, rows * top, limit, skew, True), portions_of(count, rows * top, limit, skew, False)
    places = jnp.arange(count)

    def named(lengths, turn):
        used = int((lengths > 0).sum())
        fixed = max(1, used // 4)
        shifted = fixed + (places - fixed + turn * (used - fixed)) % max(1, count - fixed)
        return jnp.zeros((count,), jnp.int32).at[order[jnp.where(places < fixed, places, shifted)]].set(jnp.asarray(lengths, jnp.int32))

    lengths = jnp.where(number % 4 == 0, named(packed, number // 4), named(ordinary, number - number // 4 - 1))
    mixed = jax.random.permutation(jax.random.fold_in(own, 3), count)
    source_of, sink = mixed[0:count // 2 * 2:2], mixed[1:count // 2 * 2:2]
    margin = jnp.minimum(lengths[source_of] - 1, limit - lengths[sink]) // 2
    margin = jnp.where((source_of == order[0]) | (sink == order[0]) | (lengths[sink] == 0), 0, jnp.maximum(margin, 0))
    shifted = jax.random.randint(jax.random.fold_in(own, 4), (count // 2,), 0, 1 << 20) % (margin + 1)
    lengths = lengths.at[source_of].add(-shifted).at[sink].add(shifted)
    items = jnp.searchsorted(jnp.cumsum(lengths), jnp.arange(rows * top), side="right").astype(jnp.int32)
    grid = items.reshape(top, rows).T
    grid = grid[jax.random.permutation(jax.random.fold_in(own, 1), rows)]
    turn = jax.random.randint(jax.random.fold_in(own, 2), (rows, 1), 0, top)
    return jnp.take_along_axis(grid, (jnp.arange(top)[None, :] + turn) % top, axis=1)


def portions_of(number_of, total, bound, lean, full):
    loads = [(1 << 20) // math.isqrt(standing ** lean) + 1 for standing in range(1, number_of + 1)]
    largest = bound if full else min(bound, max(-(-total // number_of), total * loads[0] // sum(loads)))
    least = 1 if total - largest >= number_of - 1 else 0
    counts, surplus = [largest] + [least] * (number_of - 1), total - largest - least * (number_of - 1)
    while surplus > 0:
        candidates = [i for i in range(1, number_of) if counts[i] < largest] or [i for i in range(1, number_of) if counts[i] < bound]
        mass, left = sum([loads[i] for i in candidates]), surplus
        for i in candidates:
            more = min(bound - counts[i], max(1, left * loads[i] // mass), surplus)
            counts[i] = counts[i] + more
            surplus = surplus - more
    return np.array(counts)


def normal_values(stream_key, dims, scale, reach, cuts=(), held_as=jnp.bfloat16):
    values = jax.random.normal(stream_key, dims, jnp.float32) * scale
    if len(cuts) > 0:
        values = shard_levels(stream_key, dims, cuts, -0.22, 0.18) * values
    return jnp.clip(values, min=-reach, max=reach).astype(held_as)


def setup_inputs(seed: int = 0) -> dict:
    splits = jax.random.split(jax.random.key(seed), 13)
    hidden_in = normal_values(splits[0], (SEQUENCE_COUNT, SEQUENCE_LENGTH, D), 1.0, 6.0, ((0, 2), (1, 16)))
    queries = normal_values(splits[1], (SEQUENCE_COUNT, SEQUENCE_LENGTH, D), 1.0, 6.0, ((0, 2), (1, 16)))
    keys = normal_values(splits[2], (SEQUENCE_COUNT, SEQUENCE_LENGTH, D), 1.0, 6.0, ((0, 2), (1, 16)))
    values = normal_values(splits[3], (SEQUENCE_COUNT, SEQUENCE_LENGTH, D), 1.0, 6.0, ((0, 2), (1, 16)))
    log_decay = draw_log_decay(jax.random.fold_in(splits[12], 71), 0)
    retention_gain = jnp.clip(1.0 + 0.15 * jax.random.normal(splits[5], (D,), jnp.float32), 0.25, 1.75)
    norm_gain = jnp.clip(1.0 + 0.15 * jax.random.normal(splits[6], (D,), jnp.float32), 0.25, 1.75)
    routes_keys = jax.random.split(jax.random.fold_in(splits[7], 1), SEQUENCE_COUNT * SEQUENCE_LENGTH // TOK_DEV)
    routes_turns = jax.random.permutation(jax.random.fold_in(splits[7], 3), SEQUENCE_COUNT * SEQUENCE_LENGTH // TOK_DEV)
    routes = jax.vmap(lambda own, number: deal_out(jax.random.fold_in(splits[7], 2), own, number, TOK_DEV, EXPERTS, TOP, CAP, 2))(routes_keys, routes_turns).reshape((SEQUENCE_COUNT, SEQUENCE_LENGTH, TOP))
    route_weights = jnp.clip(0.1 + 0.9 * jax.random.uniform(splits[8], (SEQUENCE_COUNT, SEQUENCE_LENGTH, TOP), jnp.float32) ** shard_levels(splits[8], (SEQUENCE_COUNT, SEQUENCE_LENGTH, TOP), ((0, 2), (1, 16)), -0.2, 0.2), 0.1, 1.0)
    w_gate = normal_values(splits[9], (EXPERTS, D, FF), D ** -0.5, 0.1875, ((0, 16), (1, 2)))
    w_up = normal_values(splits[10], (EXPERTS, D, FF), D ** -0.5, 0.1875, ((0, 16), (1, 2)))
    w_down = normal_values(splits[11], (EXPERTS, D, FF), FF ** -0.5, 0.15625, ((0, 16), (1, 2)))
    return {"hidden_in": hidden_in, "queries": queries, "keys": keys, "values": values, "log_decay": log_decay, "retention_gain": retention_gain, "norm_gain": norm_gain, "routes": routes, "route_weights": route_weights, "w_gate": w_gate, "w_up": w_up, "w_down": w_down}


def rotate(vectors, token_position):
    half_dim = vectors.shape[-1] // 2
    inverse = 10000.0 ** (-jnp.arange(half_dim, dtype=jnp.float32) / half_dim)
    angles = token_position.astype(jnp.float32)[:, None] * inverse[None, :]
    cosine = jnp.cos(angles)[:, None, :]
    sine_part = jnp.sin(angles)[:, None, :]
    leading = vectors[..., :half_dim]
    trailing = vectors[..., half_dim:]
    return jnp.concatenate([leading * cosine - trailing * sine_part, trailing * cosine + leading * sine_part], axis=-1)

def retain_block(carried_state, members):
    query_blk, key_blk, value_blk, decay_blk, token_position = members
    tok_count = query_blk.shape[0]
    per_head_queries = (rotate(query_blk.astype(jnp.float32).reshape(tok_count, RETENTION_HEADS, HK), token_position) * HK ** (-0.5)).astype(jnp.bfloat16)
    per_head_keys = rotate(key_blk.astype(jnp.float32).reshape(tok_count, RETENTION_HEADS, HK), token_position).astype(jnp.bfloat16)
    per_head_values = value_blk.reshape(tok_count, RETENTION_HEADS, HK)
    running_total = jnp.cumsum(decay_blk, axis=0)
    scores = jnp.einsum('thd,shd->hts', per_head_queries.astype(jnp.float32), per_head_keys.astype(jnp.float32))
    causal = jnp.arange(tok_count)[:, None] >= jnp.arange(tok_count)[None, :]
    spread = running_total.T[:, :, None] - running_total.T[:, None, :]
    weights = jnp.where(causal[None], scores * jnp.exp(jnp.where(causal[None], spread, 0.0)), 0.0).astype(jnp.bfloat16)
    inside = jnp.einsum('hts,shd->thd', weights.astype(jnp.float32), per_head_values.astype(jnp.float32))
    external_part = jnp.exp(running_total)[:, :, None] * jnp.einsum('wjc,jco->wjo', per_head_queries.astype(jnp.float32), carried_state, precision=lax.Precision.HIGHEST)
    trailing_decay = jnp.exp(running_total[-1][None, :] - running_total)
    block_summary = jnp.einsum('qpf,qpy->pfy', per_head_keys.astype(jnp.float32) * trailing_decay[:, :, None], per_head_values.astype(jnp.float32), precision=lax.Precision.HIGHEST)
    carried_next = jnp.exp(running_total[-1])[:, None, None] * carried_state + block_summary
    return (carried_next, (inside + external_part).reshape(tok_count, RETENTION_HEADS * HK))

def retain_sequence(members):
    query_seq, key_seq, value_seq, decay_seq = members
    blocks = SEQUENCE_LENGTH // TOK_DEV
    token_position = jnp.arange(SEQUENCE_LENGTH, dtype=jnp.int32).reshape(blocks, TOK_DEV)

    def shaped(tensor):
        return tensor.reshape((blocks, TOK_DEV) + tensor.shape[1:])
    start_state = jnp.zeros((RETENTION_HEADS, HK, HK), jnp.float32)
    final_state, retrieved = lax.scan(retain_block, start_state, (shaped(query_seq), shaped(key_seq), shaped(value_seq), shaped(decay_seq), token_position))
    return retrieved.reshape(SEQUENCE_LENGTH, RETENTION_HEADS * HK)

def reference(hidden_in, queries, keys, values, log_decay, retention_gain, norm_gain, routes, route_weights, w_gate, w_up, w_down):
    retrieved = lax.map(retain_sequence, (queries, keys, values, log_decay))
    heads_view = retrieved.reshape(SEQUENCE_COUNT, SEQUENCE_LENGTH, RETENTION_HEADS, HK)
    centre = lax.optimization_barrier(jnp.mean(heads_view, axis=-1, keepdims=True))
    deviation = heads_view - centre
    variance = lax.optimization_barrier(jnp.mean(deviation * deviation, axis=-1, keepdims=True))
    normalized = (deviation * lax.rsqrt(variance + 1e-05)).reshape(SEQUENCE_COUNT, SEQUENCE_LENGTH, D)
    residual = hidden_in.astype(jnp.float32) + retention_gain * normalized
    square_mean = lax.optimization_barrier(jnp.mean(residual * residual, axis=-1, keepdims=True))
    normed = (residual * lax.rsqrt(square_mean + 1e-06) * norm_gain).astype(jnp.bfloat16)
    total_rows = SEQUENCE_COUNT * SEQUENCE_LENGTH
    block_total = total_rows // TOK_DEV
    flat_norm = normed.reshape(total_rows, D)
    route_blocks = routes.reshape(block_total, TOK_DEV * TOP)
    weight_blocks = route_weights.reshape(block_total, TOK_DEV * TOP)
    expert_ids = jnp.arange(EXPERTS, dtype=jnp.int32)
    expert_hits = (route_blocks[:, :, None] == expert_ids[None, None, :]).astype(jnp.int32)
    earlier = jnp.cumsum(expert_hits, axis=1) - expert_hits
    slot_rank = lax.optimization_barrier(jnp.sum(earlier * expert_hits, axis=2)).astype(jnp.int32)
    slot_lanes = jnp.arange(block_total, dtype=jnp.int32)[:, None] * CAP + slot_rank
    owners = jnp.arange(block_total, dtype=jnp.int32)[:, None] * TOK_DEV + jnp.arange(TOK_DEV * TOP, dtype=jnp.int32)[None, :] // TOP
    token_table = jnp.full((EXPERTS, block_total * CAP), -1, jnp.int32).at[route_blocks, slot_lanes].set(owners)
    weight_table = jnp.zeros((EXPERTS, block_total * CAP), jnp.float32).at[route_blocks, slot_lanes].set(weight_blocks)

    def apply_expert(accumulated, members):
        token_ids, token_weights, gate_weight, up_weight, down_weight = members
        present = token_ids >= 0
        safe_ids = jnp.maximum(token_ids, 0)
        picked = flat_norm[safe_ids]
        gate_val = jnp.dot(picked, gate_weight, preferred_element_type=jnp.float32)
        up_val = jnp.dot(picked, up_weight, preferred_element_type=jnp.float32)
        hidden = (jax.nn.silu(gate_val) * up_val).astype(jnp.bfloat16)
        expert_out = jnp.dot(hidden, down_weight.T, preferred_element_type=jnp.float32).astype(jnp.bfloat16)
        contribution = jnp.where(present[:, None], expert_out.astype(jnp.float32) * token_weights[:, None], 0.0)
        return (accumulated.at[safe_ids].add(contribution), None)
    start_sum = jnp.zeros((total_rows, D), jnp.float32)
    accumulated, unused = lax.scan(apply_expert, start_sum, (token_table, weight_table, w_gate, w_up, w_down))
    output = residual.reshape(total_rows, D) + accumulated
    return output.astype(jnp.bfloat16).reshape(SEQUENCE_COUNT, SEQUENCE_LENGTH, D)
```

```python
import jax
import jax.numpy as jnp
from jax import lax
from jax.sharding import PartitionSpec as P


def carried_in(part, axis, combine, identity):
    place = lax.axis_index(axis)
    gathered = jax.tree.map(lambda a: lax.all_gather(a, axis), part)
    state = jax.tree.map(lambda a, e: jnp.zeros_like(a) + jnp.asarray(e, a.dtype), part, identity)

    def one(lap, state):
        return combine(
            state, jax.tree.map(lambda a: lax.dynamic_index_in_dim(a, lap, 0, False), gathered)
        )

    return lax.fori_loop(0, place, one, state)


def rotate(vectors, token_position):
    half_dim = vectors.shape[-1] // 2
    inverse = 10000.0 ** (-jnp.arange(half_dim, dtype=jnp.float32) / half_dim)
    angles = token_position.astype(jnp.float32)[:, None] * inverse[None, :]
    cosine = jnp.cos(angles)[:, None, :]
    sine_part = jnp.sin(angles)[:, None, :]
    leading = vectors[..., :half_dim]
    trailing = vectors[..., half_dim:]
    return jnp.concatenate(
        [leading * cosine - trailing * sine_part, trailing * cosine + leading * sine_part], axis=-1
    )


def chain_combine(earlier, later_part):
    return (earlier[0] * later_part[0], later_part[0][:, None, None] * earlier[1] + later_part[1])


def body(
    hidden_in,
    queries,
    keys,
    values,
    log_decay,
    retention_gain,
    norm_gain,
    routes,
    route_weights,
    w_gate,
    w_up,
    w_down,
):
    owner_axes = ("ctx", "dp")
    gather_axis = "exp"
    shards = (w_gate, w_up, w_down)
    if lax.axis_size("exp") == 2 and lax.axis_size("dp") == 2:
        owner_axes = ("ctx", "exp")
        gather_axis = "dp"
        shards = tuple(
            lax.ppermute(w, ("exp", "dp"), [(0, 0), (1, 2), (2, 1), (3, 3)]) for w in shards
        )
    full_gate, full_up, full_down = (
        lax.all_gather(w, gather_axis, axis=1, tiled=True)[0] for w in shards
    )
    tok_rows = hidden_in.shape[1]
    model_width = hidden_in.shape[2]
    head_count = log_decay.shape[2]
    head_dim = model_width // head_count
    block_index = lax.axis_index("ctx") * lax.axis_size("exp") + lax.axis_index("exp")
    token_position = block_index * tok_rows + jnp.arange(tok_rows, dtype=jnp.int32)
    per_head_queries = (
        rotate(
            queries[0].astype(jnp.float32).reshape(tok_rows, head_count, head_dim), token_position
        )
        * head_dim ** (-0.5)
    ).astype(jnp.bfloat16)
    per_head_keys = rotate(
        keys[0].astype(jnp.float32).reshape(tok_rows, head_count, head_dim), token_position
    ).astype(jnp.bfloat16)
    per_head_values = values[0].reshape(tok_rows, head_count, head_dim)
    running_total = jnp.cumsum(log_decay[0], axis=0)
    scores = jnp.einsum(
        "thd,shd->hts", per_head_queries, per_head_keys, preferred_element_type=jnp.float32
    )
    causal = jnp.arange(tok_rows)[:, None] >= jnp.arange(tok_rows)[None, :]
    spread = running_total.T[:, :, None] - running_total.T[:, None, :]
    weights = jnp.where(
        causal[None], scores * jnp.exp(jnp.where(causal[None], spread, 0.0)), 0.0
    ).astype(jnp.bfloat16)
    inside = jnp.einsum(
        "hts,shd->thd", weights, per_head_values, preferred_element_type=jnp.float32
    )
    trailing_decay = jnp.exp(running_total[-1][None, :] - running_total)
    block_summary = jnp.einsum(
        "qpf,qpy->pfy",
        per_head_keys.astype(jnp.float32) * trailing_decay[:, :, None],
        per_head_values.astype(jnp.float32),
        precision=lax.Precision.HIGHEST,
    )
    group_logs, group_sums = (
        lax.all_gather(running_total[-1][None], "exp", axis=0, tiled=True),
        lax.all_gather(block_summary[None], "exp", axis=0, tiled=True),
    )
    group_size = lax.axis_size("exp")
    own_member = lax.axis_index("exp")
    inclusive = jnp.cumsum(group_logs, axis=0)
    exclusive = inclusive - group_logs
    entering_log = lax.dynamic_index_in_dim(exclusive, own_member, 0, keepdims=False)
    before_me = jnp.arange(group_size, dtype=jnp.int32)[:, None] < own_member
    inner_coeff = jnp.where(
        before_me, jnp.exp(jnp.where(before_me, entering_log[None, :] - inclusive, 0.0)), 0.0
    )
    inner_state = jnp.einsum(
        "jh,jhab->hab", inner_coeff, group_sums, precision=lax.Precision.HIGHEST
    )
    total_coeff = jnp.exp(inclusive[-1][None, :] - inclusive)
    group_state = jnp.einsum(
        "jh,jhab->hab", total_coeff, group_sums, precision=lax.Precision.HIGHEST
    )
    group_decay = jnp.exp(inclusive[-1])
    identity = (
        jnp.ones((head_count,), jnp.float32),
        jnp.zeros((head_count, head_dim, head_dim), jnp.float32),
    )
    leading_sum = carried_in((group_decay, group_state), "ctx", chain_combine, identity)
    state_in = jnp.exp(entering_log)[:, None, None] * leading_sum[1] + inner_state
    external_part = jnp.exp(running_total)[:, :, None] * jnp.einsum(
        "wjc,jco->wjo",
        per_head_queries.astype(jnp.float32),
        state_in,
        precision=lax.Precision.HIGHEST,
    )
    retrieved = inside + external_part
    centre = jnp.mean(retrieved, axis=-1, keepdims=True)
    deviation = retrieved - centre
    variance = jnp.mean(deviation * deviation, axis=-1, keepdims=True)
    normalized = (deviation * lax.rsqrt(variance + 1e-05)).reshape(tok_rows, model_width)
    residual = hidden_in[0].astype(jnp.float32) + retention_gain * normalized
    square_mean = jnp.mean(residual * residual, axis=-1, keepdims=True)
    normed = (residual * lax.rsqrt(square_mean + 1e-06) * norm_gain).astype(jnp.bfloat16)
    expert_count = lax.axis_size("ctx") * lax.axis_size("dp")
    top_count = routes.shape[2]
    capacity = (tok_rows * top_count * 5 + 4 * expert_count - 1) // (4 * expert_count)
    slot_count = expert_count * capacity
    route_rows = routes[0]
    expert_hits = (
        route_rows.reshape(tok_rows * top_count)[:, None]
        == jnp.arange(expert_count, dtype=jnp.int32)[None, :]
    ).astype(jnp.int32)
    earlier = jnp.cumsum(expert_hits, axis=0) - expert_hits
    slot_rank = jnp.sum(earlier * expert_hits, axis=1).reshape(tok_rows, top_count)
    destination = route_rows * capacity + slot_rank
    slot_lanes = jnp.arange(slot_count, dtype=jnp.int32)
    placing = jnp.any(destination[None, :, :] == slot_lanes[:, None, None], axis=2).astype(
        jnp.bfloat16
    )
    outgoing = jnp.dot(placing, normed, preferred_element_type=jnp.float32).astype(jnp.bfloat16)
    arrived = lax.all_to_all(
        outgoing.reshape(expert_count, capacity, model_width),
        owner_axes,
        split_axis=0,
        concat_axis=0,
        tiled=True,
    ).reshape(slot_count, model_width)
    gate_next = jnp.dot(
        arrived,
        full_gate,
        preferred_element_type=jnp.float32,
    )
    up_next = jnp.dot(
        arrived,
        full_up,
        preferred_element_type=jnp.float32,
    )
    hidden = (jax.nn.silu(gate_next) * up_next).astype(jnp.bfloat16)
    expert_out = lax.dot_general(
        hidden,
        full_down,
        (((1,), (1,)), ((), ())),
        preferred_element_type=jnp.float32,
    ).astype(jnp.bfloat16)
    returned = lax.all_to_all(
        expert_out.reshape(expert_count, capacity, model_width),
        owner_axes,
        split_axis=0,
        concat_axis=0,
        tiled=True,
    ).reshape(slot_count, model_width)
    output = residual
    for route_index in range(top_count):
        picking = (destination[:, route_index][:, None] == slot_lanes[None, :]).astype(jnp.bfloat16)
        routed = jnp.dot(picking, returned, preferred_element_type=jnp.float32)
        output = output + route_weights[0][:, route_index][:, None] * routed
    return output.astype(jnp.bfloat16)[None]


def solution(mesh):
    in_specs = (
        P("dp", ("ctx", "exp"), None),
        P("dp", ("ctx", "exp"), None),
        P("dp", ("ctx", "exp"), None),
        P("dp", ("ctx", "exp"), None),
        P("dp", ("ctx", "exp"), None),
        P(),
        P(),
        P("dp", ("ctx", "exp"), None),
        P("dp", ("ctx", "exp"), None),
        P(("ctx", "dp"), "exp", None),
        P(("ctx", "dp"), "exp", None),
        P(("ctx", "dp"), "exp", None),
    )
    out_specs = P("dp", ("ctx", "exp"), None)
    return jax.shard_map(body, mesh=mesh, in_specs=in_specs, out_specs=out_specs, check_vma=False)
```

```python
import functools

import jax
import jax.numpy as jnp
from jax import lax
from jax.experimental import pallas as pl
from jax.experimental.pallas import tpu as pltpu
from jax.sharding import PartitionSpec as P


def carried_in(part, axis, combine, identity):
    place = lax.axis_index(axis)
    gathered = jax.tree.map(lambda a: lax.all_gather(a, axis), part)
    state = jax.tree.map(lambda a, e: jnp.zeros_like(a) + jnp.asarray(e, a.dtype), part, identity)

    def one(lap, state):
        return combine(
            state, jax.tree.map(lambda a: lax.dynamic_index_in_dim(a, lap, 0, False), gathered)
        )

    return lax.fori_loop(0, place, one, state)


def rotate(vectors, token_position):
    half_dim = vectors.shape[-1] // 2
    inverse = 10000.0 ** (-jnp.arange(half_dim, dtype=jnp.float32) / half_dim)
    angles = token_position.astype(jnp.float32)[:, None] * inverse[None, :]
    cosine = jnp.cos(angles)[:, None, :]
    sine_part = jnp.sin(angles)[:, None, :]
    leading = vectors[..., :half_dim]
    trailing = vectors[..., half_dim:]
    return jnp.concatenate(
        [leading * cosine - trailing * sine_part, trailing * cosine + leading * sine_part], axis=-1
    )


def chain_combine(earlier, later_part):
    return (earlier[0] * later_part[0], later_part[0][:, None, None] * earlier[1] + later_part[1])


def body(
    hidden_in,
    queries,
    keys,
    values,
    log_decay,
    retention_gain,
    norm_gain,
    routes,
    route_weights,
    w_gate,
    w_up,
    w_down,
):
    tok_rows = hidden_in.shape[1]
    model_width = hidden_in.shape[2]
    head_count = log_decay.shape[2]
    head_dim = model_width // head_count
    block_index = lax.axis_index("ctx") * lax.axis_size("exp") + lax.axis_index("exp")
    token_position = block_index * tok_rows + jnp.arange(tok_rows, dtype=jnp.int32)
    per_head_queries = (
        rotate(
            queries[0].astype(jnp.float32).reshape(tok_rows, head_count, head_dim), token_position
        )
        * head_dim ** (-0.5)
    ).astype(jnp.bfloat16)
    per_head_keys = rotate(
        keys[0].astype(jnp.float32).reshape(tok_rows, head_count, head_dim), token_position
    ).astype(jnp.bfloat16)
    per_head_values = values[0].reshape(tok_rows, head_count, head_dim)
    running_total = jnp.cumsum(log_decay[0], axis=0)
    scores = jnp.einsum(
        "thd,shd->hts", per_head_queries, per_head_keys, preferred_element_type=jnp.float32
    )
    causal = jnp.arange(tok_rows)[:, None] >= jnp.arange(tok_rows)[None, :]
    spread = running_total.T[:, :, None] - running_total.T[:, None, :]
    weights = jnp.where(
        causal[None], scores * jnp.exp(jnp.where(causal[None], spread, 0.0)), 0.0
    ).astype(jnp.bfloat16)
    inside = jnp.einsum(
        "hts,shd->thd", weights, per_head_values, preferred_element_type=jnp.float32
    )
    trailing_decay = jnp.exp(running_total[-1][None, :] - running_total)
    block_summary = jnp.einsum(
        "qpf,qpy->pfy",
        per_head_keys.astype(jnp.float32) * trailing_decay[:, :, None],
        per_head_values.astype(jnp.float32),
        precision=lax.Precision.HIGHEST,
    )
    group_logs, group_sums = (
        lax.all_gather(running_total[-1][None], "exp", axis=0, tiled=True),
        lax.all_gather(block_summary[None], "exp", axis=0, tiled=True),
    )
    group_size = lax.axis_size("exp")
    own_member = lax.axis_index("exp")
    inclusive = jnp.cumsum(group_logs, axis=0)
    exclusive = inclusive - group_logs
    entering_log = lax.dynamic_index_in_dim(exclusive, own_member, 0, keepdims=False)
    before_me = jnp.arange(group_size, dtype=jnp.int32)[:, None] < own_member
    inner_coeff = jnp.where(
        before_me, jnp.exp(jnp.where(before_me, entering_log[None, :] - inclusive, 0.0)), 0.0
    )
    inner_state = jnp.einsum(
        "jh,jhab->hab", inner_coeff, group_sums, precision=lax.Precision.HIGHEST
    )
    total_coeff = jnp.exp(inclusive[-1][None, :] - inclusive)
    group_state = jnp.einsum(
        "jh,jhab->hab", total_coeff, group_sums, precision=lax.Precision.HIGHEST
    )
    group_decay = jnp.exp(inclusive[-1])
    identity = (
        jnp.ones((head_count,), jnp.float32),
        jnp.zeros((head_count, head_dim, head_dim), jnp.float32),
    )
    leading_sum = carried_in((group_decay, group_state), "ctx", chain_combine, identity)
    state_in = jnp.exp(entering_log)[:, None, None] * leading_sum[1] + inner_state
    external_part = jnp.exp(running_total)[:, :, None] * jnp.einsum(
        "wjc,jco->wjo",
        per_head_queries.astype(jnp.float32),
        state_in,
        precision=lax.Precision.HIGHEST,
    )
    retrieved = inside + external_part
    centre = jnp.mean(retrieved, axis=-1, keepdims=True)
    deviation = retrieved - centre
    variance = jnp.mean(deviation * deviation, axis=-1, keepdims=True)
    normalized = (deviation * lax.rsqrt(variance + 1e-05)).reshape(tok_rows, model_width)
    residual = hidden_in[0].astype(jnp.float32) + retention_gain * normalized
    square_mean = jnp.mean(residual * residual, axis=-1, keepdims=True)
    normed = (residual * lax.rsqrt(square_mean + 1e-06) * norm_gain).astype(jnp.bfloat16)
    expert_count = lax.axis_size("ctx") * lax.axis_size("dp")
    top_count = routes.shape[2]
    capacity = (tok_rows * top_count * 5 + 4 * expert_count - 1) // (4 * expert_count)
    slot_count = expert_count * capacity
    route_rows = routes[0]
    expert_hits = (
        route_rows.reshape(tok_rows * top_count)[:, None]
        == jnp.arange(expert_count, dtype=jnp.int32)[None, :]
    ).astype(jnp.int32)
    earlier = jnp.cumsum(expert_hits, axis=0) - expert_hits
    slot_rank = jnp.sum(earlier * expert_hits, axis=1).reshape(tok_rows, top_count)
    destination = route_rows * capacity + slot_rank
    slot_lanes = jnp.arange(slot_count, dtype=jnp.int32)
    placing = jnp.any(destination[None, :, :] == slot_lanes[:, None, None], axis=2).astype(
        jnp.bfloat16
    )
    outgoing = jnp.dot(placing, normed, preferred_element_type=jnp.float32).astype(jnp.bfloat16)
    arrived = lax.all_to_all(
        outgoing.reshape(expert_count, capacity, model_width),
        ("ctx", "dp"),
        split_axis=0,
        concat_axis=0,
        tiled=True,
    ).reshape(slot_count, model_width)
    gate_next = jnp.dot(
        arrived,
        lax.all_gather(w_gate, "exp", axis=1, tiled=True)[0],
        preferred_element_type=jnp.float32,
    )
    up_next = jnp.dot(
        arrived,
        lax.all_gather(w_up, "exp", axis=1, tiled=True)[0],
        preferred_element_type=jnp.float32,
    )
    hidden = (jax.nn.silu(gate_next) * up_next).astype(jnp.bfloat16)
    expert_out = lax.dot_general(
        hidden,
        lax.all_gather(w_down, "exp", axis=1, tiled=True)[0],
        (((1,), (1,)), ((), ())),
        preferred_element_type=jnp.float32,
    ).astype(jnp.bfloat16)
    returned = lax.all_to_all(
        expert_out.reshape(expert_count, capacity, model_width),
        ("ctx", "dp"),
        split_axis=0,
        concat_axis=0,
        tiled=True,
    ).reshape(slot_count, model_width)
    output = residual
    for route_index in range(top_count):
        picking = (destination[:, route_index][:, None] == slot_lanes[None, :]).astype(jnp.bfloat16)
        routed = jnp.dot(picking, returned, preferred_element_type=jnp.float32)
        output = output + route_weights[0][:, route_index][:, None] * routed
    return output.astype(jnp.bfloat16)[None]


MESH = pl.DeviceIdType.MESH
BF16 = jnp.bfloat16
F32 = jnp.float32
TILE = 16


def iota(shape, dim):
    return lax.broadcasted_iota(jnp.int32, shape, dim)


def dot(a, b, contract=((1,), (0,)), precision=None):
    return lax.dot_general(
        a, b, (contract, ((), ())), precision=precision, preferred_element_type=F32
    )


def fused_kernel(
    geo,
    hid,
    q,
    k,
    v,
    ld,
    rgain,
    ngain,
    inv,
    routes,
    rweights,
    wg,
    wu,
    wd,
    out,
    wgb,
    wub,
    wdb,
    sum_send,
    sum_recv,
    dec_send,
    dec_recv,
    ent_send,
    ent_recv,
    disp_main,
    disp_rem,
    xall,
    xin_rem,
    hidden,
    eo_main,
    orem,
    eo_rem,
    ret_main,
    ret_rem,
    qrot,
    krot,
    resid,
    w_local,
    w_swap_send,
    w_swap_recv,
    w_sib_send,
    w_sib_recv,
    x_send,
    x_recv,
):
    ctx_n, exp_n, cap = geo
    nb = ctx_n * exp_n
    rows, width = hid.shape
    heads = ld.shape[1]
    hd = width // heads
    ff = wg.shape[1]
    half = wg.shape[0]
    rem_n = cap - TILE
    fold = TILE // rem_n
    fw = width // fold
    rp = width // nb
    x = lax.axis_index("exp")
    c = lax.axis_index("dp")
    me = lax.axis_index("ctx") * exp_n + x
    stays = c == x
    moves = c != x

    def peer(index):
        return {"ctx": index // exp_n, "exp": index % exp_n}

    sibling = {"dp": 1 - c}
    partner = {"exp": c, "dp": x}

    barrier = pltpu.get_barrier_semaphore()

    def greet(d, carry):
        pl.semaphore_signal(
            barrier, inc=1, device_id=peer(lax.rem(me + d, nb)), device_id_type=MESH
        )
        return carry

    lax.fori_loop(1, nb, greet, 0)
    pl.semaphore_signal(barrier, inc=1, device_id=sibling, device_id_type=MESH)

    @pl.when(moves)
    def _():
        pl.semaphore_signal(barrier, inc=1, device_id=partner, device_id_type=MESH)
        pl.semaphore_wait(barrier, nb + 1)

    @pl.when(stays)
    def _():
        pl.semaphore_wait(barrier, nb)

    chunks = []
    for array, (src, buf) in enumerate(((wg, wgb), (wu, wub), (wd, wdb))):
        pieces = 4 if array == 2 else 2
        step = half // pieces
        for piece in range(pieces):
            chunks.append((src, buf, piece * step, step, array))

    def place(buf, owner, start, step):
        return buf.at[pl.ds(pl.multiple_of(owner * half + start, TILE), step)]

    def swap_copy(i):
        src, buf, start, step, _ = chunks[i]
        return pltpu.make_async_remote_copy(
            src_ref=src.at[pl.ds(start, step)],
            dst_ref=place(buf, x, start, step),
            send_sem=w_swap_send.at[i],
            recv_sem=w_swap_recv.at[i],
            device_id=partner,
            device_id_type=MESH,
        )

    def swap_arrival(i):
        src, buf, start, step, _ = chunks[i]
        return pltpu.make_async_remote_copy(
            src_ref=src.at[pl.ds(start, step)],
            dst_ref=place(buf, c, start, step),
            send_sem=w_swap_send.at[i],
            recv_sem=w_swap_recv.at[i],
            device_id=partner,
            device_id_type=MESH,
        )

    def sib_copy(i, own):
        src, buf, start, step, _ = chunks[i]
        mine = place(buf, c, start, step)
        return pltpu.make_async_remote_copy(
            src_ref=src.at[pl.ds(start, step)] if own else mine,
            dst_ref=mine,
            send_sem=w_sib_send.at[i],
            recv_sem=w_sib_recv.at[i],
            device_id=sibling,
            device_id_type=MESH,
        )

    def sib_arrival(i):
        src, buf, start, step, _ = chunks[i]
        return pltpu.make_async_remote_copy(
            src_ref=src.at[pl.ds(start, step)],
            dst_ref=place(buf, 1 - c, start, step),
            send_sem=w_sib_send.at[i],
            recv_sem=w_sib_recv.at[i],
            device_id=sibling,
            device_id_type=MESH,
        )

    def local_copy(i):
        src, buf, start, step, _ = chunks[i]
        return pltpu.make_async_copy(
            src.at[pl.ds(start, step)], place(buf, c, start, step), w_local.at[i]
        )

    @pl.when(moves)
    def _():
        for i in range(len(chunks)):
            swap_copy(i).start()

    @pl.when(stays)
    def _():
        for i in range(len(chunks)):
            sib_copy(i, True).start()
            local_copy(i).start()

    def hand_on(array):
        @pl.when(moves)
        def _():
            for i in range(len(chunks)):
                if chunks[i][4] == array:
                    swap_arrival(i).wait_recv()
                    sib_copy(i, False).start()

    def take(array):
        @pl.when(stays)
        def _():
            for i in range(len(chunks)):
                if chunks[i][4] == array:
                    local_copy(i).wait()

        for i in range(len(chunks)):
            if chunks[i][4] == array:
                sib_arrival(i).wait_recv()

    def exchange(kind, src, dst, n):
        def at(ref, index):
            return ref.at[pl.ds(pl.multiple_of(index * n, n), n)]

        def copy(d, landing):
            dest = lax.rem(me + d, nb)
            return pltpu.make_async_remote_copy(
                src_ref=at(src, dest),
                dst_ref=at(dst, landing),
                send_sem=x_send.at[kind, d],
                recv_sem=x_recv.at[kind, d],
                device_id=peer(dest),
                device_id_type=MESH,
            )

        def start():
            def one(d, carry):
                copy(d, me).start()
                return carry

            lax.fori_loop(1, nb, one, 0)

        def arrive():
            def one(d, carry):
                copy(d, lax.rem(me + nb - d, nb)).wait_recv()
                return carry

            lax.fori_loop(1, nb, one, 0)

        def sent():
            def one(d, carry):
                copy(d, me).wait_send()
                return carry

            lax.fori_loop(1, nb, one, 0)

        own = pl.ds(pl.multiple_of(me * n, n), n)
        return start, arrive, sent, own

    lane = iota((rows, hd), 1)
    position = (me * rows + iota((rows, hd), 0)).astype(F32)
    angle = position * inv[...]
    cosine = jnp.cos(angle)
    sine = jnp.where(lane < hd // 2, -1.0, 1.0) * jnp.sin(angle)
    causal = iota((rows, rows), 0) >= iota((rows, rows), 1)
    lower = causal.astype(F32)
    upper = (iota((rows, rows), 0) <= iota((rows, rows), 1)).astype(F32)
    decay = ld[...]
    total = dot(lower, decay, precision=lax.Precision.HIGHEST)
    total_t = dot(decay.T, upper, precision=lax.Precision.HIGHEST)
    last_t = total_t[:, rows - 1 : rows]
    dec_send[...] = jnp.broadcast_to(jnp.exp(last_t), dec_send.shape)
    for h in range(heads):
        cols = slice(h * hd, (h + 1) * hd)
        q_h = q[:, cols].astype(F32)
        k_h = k[:, cols].astype(F32)
        q_h = (q_h * cosine + pltpu.roll(q_h, hd // 2, 1) * sine) * hd ** (-0.5)
        k_h = (k_h * cosine + pltpu.roll(k_h, hd // 2, 1) * sine).astype(BF16)
        qrot[:, cols] = q_h.astype(BF16)
        krot[:, cols] = k_h
        column = total[:, h : h + 1]
        scaled = k_h.astype(F32) * jnp.exp(total[rows - 1 : rows, h : h + 1] - column)
        scaled = scaled.T
        coarse = scaled.astype(BF16)
        fine = (scaled - coarse.astype(F32)).astype(BF16)
        v_h = v[:, cols]
        sum_send[cols, :] = (dot(coarse, v_h) + dot(fine, v_h)).astype(BF16)

    start_s, arrive_s, sent_s, own_s = exchange(0, sum_send, sum_recv, rp)

    def dec_copy(d, landing):
        dest = lax.rem(me + d, nb)
        return pltpu.make_async_remote_copy(
            src_ref=dec_send,
            dst_ref=dec_recv.at[landing],
            send_sem=x_send.at[1, d],
            recv_sem=x_recv.at[1, d],
            device_id=peer(dest),
            device_id_type=MESH,
        )

    def dec_start(d, carry):
        dec_copy(d, me).start()
        return carry

    def dec_arrive(d, carry):
        dec_copy(d, lax.rem(me + nb - d, nb)).wait_recv()
        return carry

    def dec_sent(d, carry):
        dec_copy(d, me).wait_send()
        return carry

    lax.fori_loop(1, nb, dec_start, 0)
    start_s()
    sum_recv[own_s, :] = sum_send[own_s, :]
    dec_recv[me] = dec_send[...]

    for h in range(heads):
        cols = slice(h * hd, (h + 1) * hd)
        spread = total[:, h : h + 1] - total_t[h : h + 1, :]
        scores = dot(qrot[:, cols], krot[:, cols], ((1,), (1,)))
        weights = jnp.where(causal, scores * jnp.exp(jnp.where(causal, spread, 0.0)), 0.0)
        resid[:, cols] = dot(weights.astype(BF16), v[:, cols])

    lax.fori_loop(1, nb, dec_arrive, 0)
    arrive_s()
    head = (me * rp) // hd
    state = jnp.zeros((rp, hd), F32)
    for b in range(nb):
        part = slice(b * rp, (b + 1) * rp)
        ent_send[part, :] = state.astype(BF16)
        if b < nb - 1:
            state = dec_recv[b, pl.ds(head, 1), :] * state + sum_recv[part, :].astype(F32)
    start_e, arrive_e, sent_e, own_e = exchange(2, ent_send, ent_recv, rp)
    start_e()
    ent_recv[own_e, :] = ent_send[own_e, :]

    r0 = routes[:, 0:1]
    r1 = routes[:, 1:2]
    lanes = iota((rows, 128), 1)
    hits = ((r0 == lanes) | (r1 == lanes)).astype(BF16)
    strict = (iota((rows, rows), 0) > iota((rows, rows), 1)).astype(BF16)
    before = dot(strict, hits)
    slots = iota((rows, nb * TILE), 1).astype(F32)
    pick_main, pick_rem = [], []
    for r in (r0, r1):
        rank = jnp.sum(jnp.where(r == lanes, before, 0.0), axis=1, keepdims=True)
        base = r.astype(F32) * TILE + rank
        in_main = jnp.where(rank < TILE, base, -1.0)
        in_rem = jnp.where(rank < TILE, -1.0e6, base - TILE)
        pick_main.append((in_main == slots).astype(F32))
        pick_rem.append([(in_rem + f * rem_n == slots).astype(F32) for f in range(fold)])
    put_main = (pick_main[0] + pick_main[1]).T.astype(BF16)
    put_rem = [(pick_rem[0][f] + pick_rem[1][f]).T.astype(BF16) for f in range(fold)]
    pick_main = [p.astype(BF16) for p in pick_main]
    pick_rem = [[p.astype(BF16) for p in ps] for ps in pick_rem]

    hand_on(0)

    arrive_e()
    square = jnp.zeros((rows, 1), F32)
    for h in range(heads):
        cols = slice(h * hd, (h + 1) * hd)
        carried = dot(qrot[:, cols], ent_recv[cols, :])
        got = resid[:, cols] + jnp.exp(total[:, h : h + 1]) * carried
        got = got - jnp.mean(got, axis=1, keepdims=True)
        variance = jnp.mean(got * got, axis=1, keepdims=True)
        got = got * lax.rsqrt(variance + 1e-05)
        got = hid[:, cols].astype(F32) + rgain[:, cols] * got
        resid[:, cols] = got
        square = square + jnp.sum(got * got, axis=1, keepdims=True)
    normed = (resid[...] * lax.rsqrt(square / width + 1e-06) * ngain[...]).astype(BF16)

    disp_main[...] = dot(put_main, normed).astype(BF16)
    folded = jnp.zeros((nb * TILE, fw), F32)
    for f in range(fold):
        folded = folded + dot(put_rem[f], normed[:, f * fw : (f + 1) * fw])
    disp_rem[...] = folded.astype(BF16)
    start_m, arrive_m, sent_m, own_m = exchange(3, disp_main, xall, TILE)
    start_r, arrive_r, sent_r, own_r = exchange(4, disp_rem, xin_rem, TILE)
    start_m()
    start_r()
    xall[own_m, :] = disp_main[own_m, :]
    xin_rem[own_r, :] = disp_rem[own_r, :]

    hand_on(1)
    arrive_m()
    arrive_r()
    row = iota((nb * rem_n, nb * TILE), 0)
    spot = (row // rem_n) * TILE + lax.rem(row, rem_n)
    for f in range(fold):
        unfold = (iota((nb * rem_n, nb * TILE), 1) == spot + f * rem_n).astype(F32)
        xall[nb * TILE :, f * fw : (f + 1) * fw] = dot(unfold.astype(BF16), xin_rem[...]).astype(
            BF16
        )

    take(0)
    take(1)

    def gate_up(i, carry):
        cols = pl.ds(pl.multiple_of(i * 128, 128), 128)
        both = dot(xall[...], jnp.concatenate([wgb[:, cols], wub[:, cols]], axis=1))
        gate = both[:, :128]
        hidden[:, cols] = (gate / (1.0 + jnp.exp(-gate)) * both[:, 128:]).astype(BF16)
        return carry

    lax.fori_loop(0, ff // 128, gate_up, 0)
    hand_on(2)
    take(2)
    block = 256

    def down(i, carry):
        cols = pl.ds(pl.multiple_of(i * block, block), block)
        result = dot(hidden[...], wdb[cols, :], ((1,), (1,))).astype(BF16)
        eo_main[:, cols] = result[: nb * TILE]
        orem[:, cols] = result[nb * TILE :]
        return carry

    lax.fori_loop(0, width // block, down, 0)
    start_b, arrive_b, sent_b, own_b = exchange(5, eo_main, ret_main, TILE)
    start_b()
    ret_main[own_b, :] = eo_main[own_b, :]
    column = iota((nb * TILE, nb * rem_n), 1)
    spot = (column // rem_n) * TILE + lax.rem(column, rem_n)
    folded = jnp.zeros((nb * TILE, fw), F32)
    for f in range(fold):
        refold = (iota((nb * TILE, nb * rem_n), 0) == spot + f * rem_n).astype(F32)
        folded = folded + dot(refold.astype(BF16), orem[:, f * fw : (f + 1) * fw])
    eo_rem[...] = folded.astype(BF16)
    start_q, arrive_q, sent_q, own_q = exchange(6, eo_rem, ret_rem, TILE)
    start_q()
    ret_rem[own_q, :] = eo_rem[own_q, :]

    @pl.when(moves)
    def _():
        for i in range(len(chunks)):
            swap_copy(i).wait_send()
            sib_copy(i, False).wait_send()

    @pl.when(stays)
    def _():
        for i in range(len(chunks)):
            sib_copy(i, True).wait_send()

    lax.fori_loop(1, nb, dec_sent, 0)
    sent_s()
    sent_e()
    sent_m()
    sent_r()

    arrive_b()
    arrive_q()
    for f in range(fold):
        cols = slice(f * fw, (f + 1) * fw)
        acc = resid[:, cols]
        for j in range(2):
            routed = dot(pick_main[j], ret_main[:, cols]) + dot(pick_rem[j][f], ret_rem[...])
            acc = acc + rweights[:, j : j + 1] * routed
        out[:, cols] = acc.astype(BF16)
    sent_b()
    sent_q()


def fused(geo, *args):
    (
        hidden_in,
        queries,
        keys,
        values,
        log_decay,
        retention_gain,
        norm_gain,
        routes,
        route_weights,
        w_gate,
        w_up,
        w_down,
    ) = args
    ctx_n, exp_n, cap = geo
    nb = ctx_n * exp_n
    rows, width = hidden_in.shape[1:]
    heads = log_decay.shape[2]
    hd = width // heads
    ff = w_gate.shape[2]
    rem_n = cap - TILE
    fw = width * rem_n // TILE
    rp = width // nb
    frequencies = 10000.0 ** (-jnp.arange(hd // 2, dtype=F32) / (hd // 2))
    inverse = jnp.concatenate([frequencies, frequencies])[None]
    vmem = pl.BlockSpec(memory_space=pltpu.VMEM)
    hbm = pl.BlockSpec(memory_space=pl.ANY)
    n_chunks = 8
    dma = pltpu.SemaphoreType.DMA
    out = pl.pallas_call(
        functools.partial(fused_kernel, geo),
        out_shape=jax.ShapeDtypeStruct((rows, width), BF16),
        in_specs=[vmem] * 10 + [hbm] * 3,
        out_specs=vmem,
        scratch_shapes=[
            pltpu.VMEM((width, ff), BF16),
            pltpu.VMEM((width, ff), BF16),
            pltpu.VMEM((width, ff), BF16),
            pltpu.VMEM((width, hd), BF16),
            pltpu.VMEM((width, hd), BF16),
            pltpu.VMEM((heads, hd), F32),
            pltpu.VMEM((nb, heads, hd), F32),
            pltpu.VMEM((width, hd), BF16),
            pltpu.VMEM((width, hd), BF16),
            pltpu.VMEM((nb * TILE, width), BF16),
            pltpu.VMEM((nb * TILE, fw), BF16),
            pltpu.VMEM((nb * cap, width), BF16),
            pltpu.VMEM((nb * TILE, fw), BF16),
            pltpu.VMEM((nb * cap, ff), BF16),
            pltpu.VMEM((nb * TILE, width), BF16),
            pltpu.VMEM((nb * rem_n, width), BF16),
            pltpu.VMEM((nb * TILE, fw), BF16),
            pltpu.VMEM((nb * TILE, width), BF16),
            pltpu.VMEM((nb * TILE, fw), BF16),
            pltpu.VMEM((rows, width), BF16),
            pltpu.VMEM((rows, width), BF16),
            pltpu.VMEM((rows, width), F32),
            dma((n_chunks,)),
            dma((n_chunks,)),
            dma((n_chunks,)),
            dma((n_chunks,)),
            dma((n_chunks,)),
            dma((7, nb)),
            dma((7, nb)),
        ],
        compiler_params=pltpu.CompilerParams(
            collective_id=0, has_side_effects=True, vmem_limit_bytes=48 * 1024 * 1024
        ),
    )(
        hidden_in[0],
        queries[0],
        keys[0],
        values[0],
        log_decay[0],
        retention_gain[None],
        norm_gain[None],
        inverse,
        routes[0],
        route_weights[0],
        w_gate[0],
        w_up[0],
        w_down[0],
    )
    return out[None]


def geometry(args):
    ctx_n, exp_n, dp_n = (lax.axis_size(a) for a in ("ctx", "exp", "dp"))
    nb = ctx_n * exp_n
    rows, width = args[0].shape[1:]
    heads = args[4].shape[2]
    hd = width // heads
    top = args[7].shape[2]
    experts = ctx_n * dp_n
    cap = (rows * top * 5 + 4 * experts - 1) // (4 * experts)
    rem_n = cap - TILE
    fits = (
        exp_n == 2
        and dp_n == 2
        and top == 2
        and experts <= 128
        and 0 < rem_n < TILE
        and TILE % rem_n == 0
        and (width * rem_n) % (TILE * 128) == 0
        and nb * rem_n % TILE == 0
        and hd == 128
        and rows == 128
        and heads == 8
        and width % nb == 0
        and (width // nb) % TILE == 0
        and hd % (width // nb) == 0
        and args[9].shape[2] % 128 == 0
        and width % 256 == 0
        and args[9].shape[1] * 2 == width
    )
    return (ctx_n, exp_n, cap) if fits else None


def layer(*args):
    geo = geometry(args)
    return body(*args) if geo is None else fused(geo, *args)


def solution(mesh):
    in_specs = (
        P("dp", ("ctx", "exp"), None),
        P("dp", ("ctx", "exp"), None),
        P("dp", ("ctx", "exp"), None),
        P("dp", ("ctx", "exp"), None),
        P("dp", ("ctx", "exp"), None),
        P(),
        P(),
        P("dp", ("ctx", "exp"), None),
        P("dp", ("ctx", "exp"), None),
        P(("ctx", "dp"), "exp", None),
        P(("ctx", "dp"), "exp", None),
        P(("ctx", "dp"), "exp", None),
    )
    out_specs = P("dp", ("ctx", "exp"), None)
    return jax.shard_map(layer, mesh=mesh, in_specs=in_specs, out_specs=out_specs, check_vma=False)
```

```python
import functools
import math

import jax
import jax.numpy as jnp
from jax import lax
from jax.experimental import pallas as pl
from jax.experimental.pallas import tpu as pltpu
from jax.sharding import PartitionSpec as P


def carried_in(part, axis, combine, identity):
    place = lax.axis_index(axis)
    gathered = jax.tree.map(lambda a: lax.all_gather(a, axis), part)
    state = jax.tree.map(lambda a, e: jnp.zeros_like(a) + jnp.asarray(e, a.dtype), part, identity)

    def one(lap, state):
        return combine(
            state, jax.tree.map(lambda a: lax.dynamic_index_in_dim(a, lap, 0, False), gathered)
        )

    return lax.fori_loop(0, place, one, state)


def rotate(vectors, token_position):
    half_dim = vectors.shape[-1] // 2
    inverse = 10000.0 ** (-jnp.arange(half_dim, dtype=jnp.float32) / half_dim)
    angles = token_position.astype(jnp.float32)[:, None] * inverse[None, :]
    cosine = jnp.cos(angles)[:, None, :]
    sine_part = jnp.sin(angles)[:, None, :]
    leading = vectors[..., :half_dim]
    trailing = vectors[..., half_dim:]
    return jnp.concatenate(
        [leading * cosine - trailing * sine_part, trailing * cosine + leading * sine_part], axis=-1
    )


def chain_combine(earlier, later_part):
    return (earlier[0] * later_part[0], later_part[0][:, None, None] * earlier[1] + later_part[1])


def body(
    hidden_in,
    queries,
    keys,
    values,
    log_decay,
    retention_gain,
    norm_gain,
    routes,
    route_weights,
    w_gate,
    w_up,
    w_down,
):
    tok_rows = hidden_in.shape[1]
    model_width = hidden_in.shape[2]
    head_count = log_decay.shape[2]
    head_dim = model_width // head_count
    block_index = lax.axis_index("ctx") * lax.axis_size("exp") + lax.axis_index("exp")
    token_position = block_index * tok_rows + jnp.arange(tok_rows, dtype=jnp.int32)
    per_head_queries = (
        rotate(
            queries[0].astype(jnp.float32).reshape(tok_rows, head_count, head_dim), token_position
        )
        * head_dim ** (-0.5)
    ).astype(jnp.bfloat16)
    per_head_keys = rotate(
        keys[0].astype(jnp.float32).reshape(tok_rows, head_count, head_dim), token_position
    ).astype(jnp.bfloat16)
    per_head_values = values[0].reshape(tok_rows, head_count, head_dim)
    running_total = jnp.cumsum(log_decay[0], axis=0)
    scores = jnp.einsum(
        "thd,shd->hts", per_head_queries, per_head_keys, preferred_element_type=jnp.float32
    )
    causal = jnp.arange(tok_rows)[:, None] >= jnp.arange(tok_rows)[None, :]
    spread = running_total.T[:, :, None] - running_total.T[:, None, :]
    weights = jnp.where(
        causal[None], scores * jnp.exp(jnp.where(causal[None], spread, 0.0)), 0.0
    ).astype(jnp.bfloat16)
    inside = jnp.einsum(
        "hts,shd->thd", weights, per_head_values, preferred_element_type=jnp.float32
    )
    trailing_decay = jnp.exp(running_total[-1][None, :] - running_total)
    block_summary = jnp.einsum(
        "qpf,qpy->pfy",
        per_head_keys.astype(jnp.float32) * trailing_decay[:, :, None],
        per_head_values.astype(jnp.float32),
        precision=lax.Precision.HIGHEST,
    )
    group_logs, group_sums = (
        lax.all_gather(running_total[-1][None], "exp", axis=0, tiled=True),
        lax.all_gather(block_summary[None], "exp", axis=0, tiled=True),
    )
    group_size = lax.axis_size("exp")
    own_member = lax.axis_index("exp")
    inclusive = jnp.cumsum(group_logs, axis=0)
    exclusive = inclusive - group_logs
    entering_log = lax.dynamic_index_in_dim(exclusive, own_member, 0, keepdims=False)
    before_me = jnp.arange(group_size, dtype=jnp.int32)[:, None] < own_member
    inner_coeff = jnp.where(
        before_me, jnp.exp(jnp.where(before_me, entering_log[None, :] - inclusive, 0.0)), 0.0
    )
    inner_state = jnp.einsum(
        "jh,jhab->hab", inner_coeff, group_sums, precision=lax.Precision.HIGHEST
    )
    total_coeff = jnp.exp(inclusive[-1][None, :] - inclusive)
    group_state = jnp.einsum(
        "jh,jhab->hab", total_coeff, group_sums, precision=lax.Precision.HIGHEST
    )
    group_decay = jnp.exp(inclusive[-1])
    identity = (
        jnp.ones((head_count,), jnp.float32),
        jnp.zeros((head_count, head_dim, head_dim), jnp.float32),
    )
    leading_sum = carried_in((group_decay, group_state), "ctx", chain_combine, identity)
    state_in = jnp.exp(entering_log)[:, None, None] * leading_sum[1] + inner_state
    external_part = jnp.exp(running_total)[:, :, None] * jnp.einsum(
        "wjc,jco->wjo",
        per_head_queries.astype(jnp.float32),
        state_in,
        precision=lax.Precision.HIGHEST,
    )
    retrieved = inside + external_part
    centre = jnp.mean(retrieved, axis=-1, keepdims=True)
    deviation = retrieved - centre
    variance = jnp.mean(deviation * deviation, axis=-1, keepdims=True)
    normalized = (deviation * lax.rsqrt(variance + 1e-05)).reshape(tok_rows, model_width)
    residual = hidden_in[0].astype(jnp.float32) + retention_gain * normalized
    square_mean = jnp.mean(residual * residual, axis=-1, keepdims=True)
    normed = (residual * lax.rsqrt(square_mean + 1e-06) * norm_gain).astype(jnp.bfloat16)
    expert_count = lax.axis_size("ctx") * lax.axis_size("dp")
    top_count = routes.shape[2]
    capacity = (tok_rows * top_count * 5 + 4 * expert_count - 1) // (4 * expert_count)
    slot_count = expert_count * capacity
    route_rows = routes[0]
    expert_hits = (
        route_rows.reshape(tok_rows * top_count)[:, None]
        == jnp.arange(expert_count, dtype=jnp.int32)[None, :]
    ).astype(jnp.int32)
    earlier = jnp.cumsum(expert_hits, axis=0) - expert_hits
    slot_rank = jnp.sum(earlier * expert_hits, axis=1).reshape(tok_rows, top_count)
    destination = route_rows * capacity + slot_rank
    slot_lanes = jnp.arange(slot_count, dtype=jnp.int32)
    placing = jnp.any(destination[None, :, :] == slot_lanes[:, None, None], axis=2).astype(
        jnp.bfloat16
    )
    outgoing = jnp.dot(placing, normed, preferred_element_type=jnp.float32).astype(jnp.bfloat16)
    arrived = lax.all_to_all(
        outgoing.reshape(expert_count, capacity, model_width),
        ("ctx", "dp"),
        split_axis=0,
        concat_axis=0,
        tiled=True,
    ).reshape(slot_count, model_width)
    gate_next = jnp.dot(
        arrived,
        lax.all_gather(w_gate, "exp", axis=1, tiled=True)[0],
        preferred_element_type=jnp.float32,
    )
    up_next = jnp.dot(
        arrived,
        lax.all_gather(w_up, "exp", axis=1, tiled=True)[0],
        preferred_element_type=jnp.float32,
    )
    hidden = (jax.nn.silu(gate_next) * up_next).astype(jnp.bfloat16)
    expert_out = lax.dot_general(
        hidden,
        lax.all_gather(w_down, "exp", axis=1, tiled=True)[0],
        (((1,), (1,)), ((), ())),
        preferred_element_type=jnp.float32,
    ).astype(jnp.bfloat16)
    returned = lax.all_to_all(
        expert_out.reshape(expert_count, capacity, model_width),
        ("ctx", "dp"),
        split_axis=0,
        concat_axis=0,
        tiled=True,
    ).reshape(slot_count, model_width)
    output = residual
    for route_index in range(top_count):
        picking = (destination[:, route_index][:, None] == slot_lanes[None, :]).astype(jnp.bfloat16)
        routed = jnp.dot(picking, returned, preferred_element_type=jnp.float32)
        output = output + route_weights[0][:, route_index][:, None] * routed
    return output.astype(jnp.bfloat16)[None]


MESH = pl.DeviceIdType.MESH
BF16 = jnp.bfloat16
F32 = jnp.float32
TILE = 16


def iota(shape, dim):
    return lax.broadcasted_iota(jnp.int32, shape, dim)


def dot(a, b, contract=((1,), (0,)), precision=None):
    return lax.dot_general(
        a, b, (contract, ((), ())), precision=precision, preferred_element_type=F32
    )


def fused_kernel(
    geo,
    hid_in,
    q_in,
    k_in,
    v_in,
    ld_in,
    rgain_in,
    ngain_in,
    routes_in,
    rweights_in,
    wg,
    wu,
    wd,
    out,
    hid,
    q,
    k,
    v,
    ld,
    rgain,
    ngain,
    routes,
    rweights,
    wgb,
    wub,
    wdb,
    sum_send,
    sum_recv,
    dec_send,
    dec_recv,
    ent_send,
    ent_recv,
    disp,
    xin,
    xall,
    hidden,
    orem,
    eo,
    ret,
    qrot,
    krot,
    resid,
    in_sem,
    w_local,
    w_swap_send,
    w_swap_recv,
    w_sib_send,
    w_sib_recv,
    x_send,
    x_recv,
):
    ctx_n, exp_n, cap = geo
    nb = ctx_n * exp_n
    rows, width = hid.shape
    heads = ld.shape[0]
    hd = width // heads
    ff = wg.shape[1]
    half = wg.shape[0]
    rem_n = cap - TILE
    fold = TILE // rem_n
    fw = width // fold
    rp = width // nb
    x = lax.axis_index("exp")
    c = lax.axis_index("dp")
    me = lax.axis_index("ctx") * exp_n + x
    stays = c == x
    moves = c != x

    def peer(index):
        return {"ctx": index // exp_n, "exp": index % exp_n}

    sibling = {"dp": 1 - c}
    partner = {"exp": c, "dp": x}

    arguments = [
        pltpu.make_async_copy(src, dst, in_sem.at[i])
        for i, (src, dst) in enumerate(
            (
                (ld_in, ld),
                (k_in, k),
                (v_in, v),
                (q_in, q),
                (routes_in, routes),
                (hid_in, hid),
                (rgain_in, rgain),
                (ngain_in, ngain),
                (rweights_in, rweights),
            )
        )
    ]
    for argument in arguments:
        argument.start()

    barrier = pltpu.get_barrier_semaphore()

    def greet(d, carry):
        pl.semaphore_signal(
            barrier, inc=1, device_id=peer(lax.rem(me + d, nb)), device_id_type=MESH
        )
        return carry

    lax.fori_loop(1, nb, greet, 0)
    pl.semaphore_signal(barrier, inc=1, device_id=sibling, device_id_type=MESH)

    @pl.when(moves)
    def _():
        pl.semaphore_signal(barrier, inc=1, device_id=partner, device_id_type=MESH)

    lane = iota((rows, hd), 1)
    pair = jnp.where(lane < hd // 2, lane, lane - hd // 2).astype(F32)
    position = (me * rows + iota((rows, hd), 0)).astype(F32)
    angle = position * jnp.exp(pair * (-math.log(10000.0) / (hd // 2)))
    cosine = jnp.cos(angle)
    sine = jnp.where(lane < hd // 2, -1.0, 1.0) * jnp.sin(angle)

    @pl.when(moves)
    def _():
        pl.semaphore_wait(barrier, nb + 1)

    @pl.when(stays)
    def _():
        pl.semaphore_wait(barrier, nb)

    chunks = []
    for array, (src, buf) in enumerate(((wg, wgb), (wu, wub), (wd, wdb))):
        pieces = 4 if array == 2 else 2
        step = half // pieces
        for piece in range(pieces):
            chunks.append((src, buf, piece * step, step, array))

    def place(buf, owner, start, step):
        return buf.at[pl.ds(pl.multiple_of(owner * half + start, TILE), step)]

    def swap_copy(i):
        src, buf, start, step, _ = chunks[i]
        return pltpu.make_async_remote_copy(
            src_ref=src.at[pl.ds(start, step)],
            dst_ref=place(buf, x, start, step),
            send_sem=w_swap_send.at[i],
            recv_sem=w_swap_recv.at[i],
            device_id=partner,
            device_id_type=MESH,
        )

    def swap_arrival(i):
        src, buf, start, step, _ = chunks[i]
        return pltpu.make_async_remote_copy(
            src_ref=src.at[pl.ds(start, step)],
            dst_ref=place(buf, c, start, step),
            send_sem=w_swap_send.at[i],
            recv_sem=w_swap_recv.at[i],
            device_id=partner,
            device_id_type=MESH,
        )

    def sib_copy(i, own):
        src, buf, start, step, _ = chunks[i]
        mine = place(buf, c, start, step)
        return pltpu.make_async_remote_copy(
            src_ref=src.at[pl.ds(start, step)] if own else mine,
            dst_ref=mine,
            send_sem=w_sib_send.at[i],
            recv_sem=w_sib_recv.at[i],
            device_id=sibling,
            device_id_type=MESH,
        )

    def sib_arrival(i):
        src, buf, start, step, _ = chunks[i]
        return pltpu.make_async_remote_copy(
            src_ref=src.at[pl.ds(start, step)],
            dst_ref=place(buf, 1 - c, start, step),
            send_sem=w_sib_send.at[i],
            recv_sem=w_sib_recv.at[i],
            device_id=sibling,
            device_id_type=MESH,
        )

    def local_copy(i):
        src, buf, start, step, _ = chunks[i]
        return pltpu.make_async_copy(
            src.at[pl.ds(start, step)], place(buf, c, start, step), w_local.at[i]
        )

    def begin(first, last):
        @pl.when(moves)
        def _():
            for i in range(first, last):
                swap_copy(i).start()

        @pl.when(stays)
        def _():
            for i in range(first, last):
                sib_copy(i, True).start()
                local_copy(i).start()

    begin(0, 1)

    def chosen(array, group):
        found = [i for i in range(len(chunks)) if chunks[i][4] == array]
        if group is None:
            return found
        share = len(found) // 2
        return found[group * share : (group + 1) * share]

    def hand_on(array, group=None):
        @pl.when(moves)
        def _():
            for i in chosen(array, group):
                swap_arrival(i).wait_recv()
                sib_copy(i, False).start()

    def take(array, group=None):
        @pl.when(stays)
        def _():
            for i in chosen(array, group):
                local_copy(i).wait()

        for i in chosen(array, group):
            sib_arrival(i).wait_recv()

    def exchange(kind, src, dst, n):
        def at(ref, index):
            return ref.at[pl.ds(pl.multiple_of(index * n, n), n)]

        def copy(d, landing):
            dest = lax.rem(me + d, nb)
            return pltpu.make_async_remote_copy(
                src_ref=at(src, dest),
                dst_ref=at(dst, landing),
                send_sem=x_send.at[kind, d],
                recv_sem=x_recv.at[kind, d],
                device_id=peer(dest),
                device_id_type=MESH,
            )

        def start():
            def one(d, carry):
                copy(d, me).start()
                return carry

            lax.fori_loop(1, nb, one, 0)

        def arrive():
            def one(d, carry):
                copy(d, lax.rem(me + nb - d, nb)).wait_recv()
                return carry

            lax.fori_loop(1, nb, one, 0)

        def sent():
            def one(d, carry):
                copy(d, me).wait_send()
                return carry

            lax.fori_loop(1, nb, one, 0)

        own = pl.ds(pl.multiple_of(me * n, n), n)
        return start, arrive, sent, own

    causal = iota((rows, rows), 0) >= iota((rows, rows), 1)
    upper = (iota((rows, rows), 0) <= iota((rows, rows), 1)).astype(F32)
    for argument in arguments[:4]:
        argument.wait()
    total_t = dot(ld[...], upper, precision=lax.Precision.HIGHEST)
    total = total_t.T
    last_t = total_t[:, rows - 1 : rows]
    dec_send[...] = jnp.broadcast_to(jnp.exp(last_t), dec_send.shape)
    for h in range(heads):
        cols = slice(h * hd, (h + 1) * hd)
        q_h = q[:, cols].astype(F32)
        k_h = k[:, cols].astype(F32)
        q_h = (q_h * cosine + pltpu.roll(q_h, hd // 2, 1) * sine) * hd ** (-0.5)
        k_h = (k_h * cosine + pltpu.roll(k_h, hd // 2, 1) * sine).astype(BF16)
        qrot[:, cols] = q_h.astype(BF16)
        krot[:, cols] = k_h
        column = total[:, h : h + 1]
        scaled = k_h.astype(F32) * jnp.exp(total[rows - 1 : rows, h : h + 1] - column)
        scaled = scaled.T
        coarse = scaled.astype(BF16)
        fine = (scaled - coarse.astype(F32)).astype(BF16)
        v_h = v[:, cols]
        sum_send[cols, :] = (dot(coarse, v_h) + dot(fine, v_h)).astype(BF16)

    start_s, arrive_s, sent_s, own_s = exchange(0, sum_send, sum_recv, rp)

    def dec_copy(d, landing):
        dest = lax.rem(me + d, nb)
        return pltpu.make_async_remote_copy(
            src_ref=dec_send,
            dst_ref=dec_recv.at[landing],
            send_sem=x_send.at[1, d],
            recv_sem=x_recv.at[1, d],
            device_id=peer(dest),
            device_id_type=MESH,
        )

    def dec_start(d, carry):
        dec_copy(d, me).start()
        return carry

    def dec_arrive(d, carry):
        dec_copy(d, lax.rem(me + nb - d, nb)).wait_recv()
        return carry

    def dec_sent(d, carry):
        dec_copy(d, me).wait_send()
        return carry

    lax.fori_loop(1, nb, dec_start, 0)
    start_s()
    begin(1, 2)
    sum_recv[own_s, :] = sum_send[own_s, :]
    dec_recv[me] = dec_send[...]

    for h in range(heads):
        cols = slice(h * hd, (h + 1) * hd)
        spread = total[:, h : h + 1] - total_t[h : h + 1, :]
        scores = dot(qrot[:, cols], krot[:, cols], ((1,), (1,)))
        weights = jnp.where(causal, scores * jnp.exp(jnp.where(causal, spread, 0.0)), 0.0)
        resid[:, cols] = dot(weights.astype(BF16), v[:, cols])

    lax.fori_loop(1, nb, dec_arrive, 0)
    arrive_s()
    head = (me * rp) // hd
    state = jnp.zeros((rp, hd), F32)
    for b in range(nb):
        part = slice(b * rp, (b + 1) * rp)
        ent_send[part, :] = state.astype(BF16)
        if b < nb - 1:
            state = dec_recv[b, pl.ds(head, 1), :] * state + sum_recv[part, :].astype(F32)
    start_e, arrive_e, sent_e, own_e = exchange(2, ent_send, ent_recv, rp)
    start_e()
    begin(2, 4)
    for argument in arguments[4:]:
        argument.wait()
    ent_recv[own_e, :] = ent_send[own_e, :]

    by_position = jnp.concatenate(
        [routes[...].astype(F32), rweights[...], jnp.zeros((4, rows), F32)], axis=0
    ).T
    r0 = by_position[:, 0:1]
    r1 = by_position[:, 1:2]
    lanes = iota((rows, 128), 1).astype(F32)
    hits = ((r0 == lanes) | (r1 == lanes)).astype(BF16)
    strict = (iota((rows, rows), 0) > iota((rows, rows), 1)).astype(BF16)
    before = dot(strict, hits)
    slots = iota((rows, nb * TILE), 1).astype(F32)
    pick_main, pick_rem = [], []
    for r in (r0, r1):
        rank = jnp.sum(jnp.where(r == lanes, before, 0.0), axis=1, keepdims=True)
        base = r * TILE + rank
        in_main = jnp.where(rank < TILE, base, -1.0)
        in_rem = jnp.where(rank < TILE, -1.0e6, base - TILE)
        pick_main.append((in_main == slots).astype(F32))
        pick_rem.append([(in_rem + f * rem_n == slots).astype(F32) for f in range(fold)])
    put_main = (pick_main[0] + pick_main[1]).T.astype(BF16)
    put_rem = [(pick_rem[0][f] + pick_rem[1][f]).T.astype(BF16) for f in range(fold)]
    pick_main = [p.astype(BF16) for p in pick_main]
    pick_rem = [[p.astype(BF16) for p in ps] for ps in pick_rem]

    arrive_e()
    square = jnp.zeros((rows, 1), F32)
    for h in range(heads):
        cols = slice(h * hd, (h + 1) * hd)
        carried = dot(qrot[:, cols], ent_recv[cols, :])
        got = resid[:, cols] + jnp.exp(total[:, h : h + 1]) * carried
        got = got - jnp.mean(got, axis=1, keepdims=True)
        variance = jnp.mean(got * got, axis=1, keepdims=True)
        got = got * lax.rsqrt(variance + 1e-05)
        got = hid[:, cols].astype(F32) + rgain[:, cols] * got
        resid[:, cols] = got
        square = square + jnp.sum(got * got, axis=1, keepdims=True)
    normed = (resid[...] * lax.rsqrt(square / width + 1e-06) * ngain[...]).astype(BF16)

    disp[:, :width] = dot(put_main, normed).astype(BF16)
    folded = jnp.zeros((nb * TILE, fw), F32)
    for f in range(fold):
        folded = folded + dot(put_rem[f], normed[:, f * fw : (f + 1) * fw])
    disp[:, width:] = folded.astype(BF16)
    start_m, arrive_m, sent_m, own_m = exchange(3, disp, xin, TILE)
    start_m()
    begin(4, 8)
    xin[own_m, :] = disp[own_m, :]

    hand_on(0)
    hand_on(1)
    arrive_m()
    xall[: nb * TILE, :] = xin[:, :width]
    row = iota((nb * rem_n, nb * TILE), 0)
    spot = (row // rem_n) * TILE + lax.rem(row, rem_n)
    for f in range(fold):
        unfold = (iota((nb * rem_n, nb * TILE), 1) == spot + f * rem_n).astype(F32)
        xall[nb * TILE :, f * fw : (f + 1) * fw] = dot(unfold.astype(BF16), xin[:, width:]).astype(
            BF16
        )

    take(0)
    take(1)

    def gate_up(i, carry):
        cols = pl.ds(pl.multiple_of(i * 128, 128), 128)
        both = dot(xall[...], jnp.concatenate([wgb[:, cols], wub[:, cols]], axis=1))
        gate = both[:, :128]
        hidden[:, cols] = (gate / (1.0 + jnp.exp(-gate)) * both[:, 128:]).astype(BF16)
        return carry

    lax.fori_loop(0, ff // 128, gate_up, 0)
    groups = 2
    part_w = half // groups
    gw = 2 * part_w
    pw = fw // groups
    column = iota((nb * TILE, nb * rem_n), 1)
    spot = (column // rem_n) * TILE + lax.rem(column, rem_n)
    returns = []
    for g in range(groups):
        hand_on(2, g)
        take(2, g)

        def down(i, carry):
            src = pl.ds(pl.multiple_of(i * half + g * part_w, part_w), part_w)
            cols = pl.ds(pl.multiple_of(i * part_w, part_w), part_w)
            result = dot(hidden[...], wdb[src, :], ((1,), (1,))).astype(BF16)
            eo[g, :, cols] = result[: nb * TILE]
            orem[:, cols] = result[nb * TILE :]
            return carry

        lax.fori_loop(0, 2, down, 0)
        folded = jnp.zeros((nb * TILE, pw), F32)
        for f in range(fold):
            refold = (iota((nb * TILE, nb * rem_n), 0) == spot + f * rem_n).astype(F32)
            folded = folded + dot(refold.astype(BF16), orem[:, f * pw : (f + 1) * pw])
        eo[g, :, gw:] = folded.astype(BF16)
        start_b, arrive_b, sent_b, own_b = exchange(4 + g, eo.at[g], ret.at[g], TILE)
        start_b()
        ret[g, own_b, :] = eo[g, own_b, :]
        returns.append((arrive_b, sent_b))

    @pl.when(moves)
    def _():
        for i in range(len(chunks)):
            swap_copy(i).wait_send()
            sib_copy(i, False).wait_send()

    @pl.when(stays)
    def _():
        for i in range(len(chunks)):
            sib_copy(i, True).wait_send()

    lax.fori_loop(1, nb, dec_sent, 0)
    sent_s()
    sent_e()
    sent_m()

    for g in range(groups):
        arrive_b, sent_b = returns[g]
        arrive_b()
        for f in range(fold):
            start = f * pw
            into = (start // part_w) * half + g * part_w + start % part_w
            cols = slice(into, into + pw)
            acc = resid[:, cols]
            for j in range(2):
                routed = dot(pick_main[j], ret[g, :, start : start + pw])
                routed = routed + dot(pick_rem[j][f], ret[g, :, gw:])
                acc = acc + by_position[:, 2 + j : 3 + j] * routed
            out[:, cols] = acc.astype(BF16)
    for arrive_b, sent_b in returns:
        sent_b()


def fused(geo, *args):
    (
        hidden_in,
        queries,
        keys,
        values,
        log_decay,
        retention_gain,
        norm_gain,
        routes,
        route_weights,
        w_gate,
        w_up,
        w_down,
    ) = args
    ctx_n, exp_n, cap = geo
    nb = ctx_n * exp_n
    rows, width = hidden_in.shape[1:]
    heads = log_decay.shape[2]
    hd = width // heads
    ff = w_gate.shape[2]
    rem_n = cap - TILE
    fw = width * rem_n // TILE
    rp = width // nb
    vmem = pl.BlockSpec(memory_space=pltpu.VMEM)
    hbm = pl.BlockSpec(memory_space=pl.ANY)
    n_chunks = 8
    dma = pltpu.SemaphoreType.DMA
    out = pl.pallas_call(
        functools.partial(fused_kernel, geo),
        out_shape=jax.ShapeDtypeStruct((rows, width), BF16),
        in_specs=[hbm] * 12,
        out_specs=vmem,
        scratch_shapes=[
            pltpu.VMEM((rows, width), BF16),
            pltpu.VMEM((rows, width), BF16),
            pltpu.VMEM((rows, width), BF16),
            pltpu.VMEM((rows, width), BF16),
            pltpu.VMEM((heads, rows), F32),
            pltpu.VMEM((1, width), F32),
            pltpu.VMEM((1, width), F32),
            pltpu.VMEM((2, rows), jnp.int32),
            pltpu.VMEM((2, rows), F32),
            pltpu.VMEM((width, ff), BF16),
            pltpu.VMEM((width, ff), BF16),
            pltpu.VMEM((width, ff), BF16),
            pltpu.VMEM((width, hd), BF16),
            pltpu.VMEM((width, hd), BF16),
            pltpu.VMEM((heads, hd), F32),
            pltpu.VMEM((nb, heads, hd), F32),
            pltpu.VMEM((width, hd), BF16),
            pltpu.VMEM((width, hd), BF16),
            pltpu.VMEM((nb * TILE, width + fw), BF16),
            pltpu.VMEM((nb * TILE, width + fw), BF16),
            pltpu.VMEM((nb * cap, width), BF16),
            pltpu.VMEM((nb * cap, ff), BF16),
            pltpu.VMEM((nb * rem_n, width // 2), BF16),
            pltpu.VMEM((2, nb * TILE, (width + fw) // 2), BF16),
            pltpu.VMEM((2, nb * TILE, (width + fw) // 2), BF16),
            pltpu.VMEM((rows, width), BF16),
            pltpu.VMEM((rows, width), BF16),
            pltpu.VMEM((rows, width), F32),
            dma((9,)),
            dma((n_chunks,)),
            dma((n_chunks,)),
            dma((n_chunks,)),
            dma((n_chunks,)),
            dma((n_chunks,)),
            dma((6, nb)),
            dma((6, nb)),
        ],
        compiler_params=pltpu.CompilerParams(
            collective_id=0, has_side_effects=True, vmem_limit_bytes=63 * 1024 * 1024
        ),
    )(
        hidden_in[0],
        queries[0],
        keys[0],
        values[0],
        log_decay[0].T,
        retention_gain[None],
        norm_gain[None],
        routes[0].T,
        route_weights[0].T,
        w_gate[0],
        w_up[0],
        w_down[0],
    )
    return out[None]


def geometry(args):
    ctx_n, exp_n, dp_n = (lax.axis_size(a) for a in ("ctx", "exp", "dp"))
    nb = ctx_n * exp_n
    rows, width = args[0].shape[1:]
    heads = args[4].shape[2]
    hd = width // heads
    top = args[7].shape[2]
    experts = ctx_n * dp_n
    cap = (rows * top * 5 + 4 * experts - 1) // (4 * experts)
    rem_n = cap - TILE
    fits = (
        exp_n == 2
        and dp_n == 2
        and top == 2
        and experts <= 128
        and 0 < rem_n < TILE
        and TILE % rem_n == 0
        and (width * rem_n) % (TILE * 256) == 0
        and rem_n * 2 <= TILE
        and nb * rem_n % TILE == 0
        and hd == 128
        and rows == 128
        and heads == 8
        and width % nb == 0
        and (width // nb) % TILE == 0
        and hd % (width // nb) == 0
        and args[9].shape[2] % 128 == 0
        and width % 256 == 0
        and args[9].shape[1] * 2 == width
    )
    return (ctx_n, exp_n, cap) if fits else None


def layer(*args):
    geo = geometry(args)
    return body(*args) if geo is None else fused(geo, *args)


def solution(mesh):
    in_specs = (
        P("dp", ("ctx", "exp"), None),
        P("dp", ("ctx", "exp"), None),
        P("dp", ("ctx", "exp"), None),
        P("dp", ("ctx", "exp"), None),
        P("dp", ("ctx", "exp"), None),
        P(),
        P(),
        P("dp", ("ctx", "exp"), None),
        P("dp", ("ctx", "exp"), None),
        P(("ctx", "dp"), "exp", None),
        P(("ctx", "dp"), "exp", None),
        P(("ctx", "dp"), "exp", None),
    )
    out_specs = P("dp", ("ctx", "exp"), None)
    return jax.shard_map(layer, mesh=mesh, in_specs=in_specs, out_specs=out_specs, check_vma=False)
```

```python
import functools
import math

import jax
import jax.numpy as jnp
from jax import lax
from jax.experimental import pallas as pl
from jax.experimental.pallas import tpu as pltpu
from jax.sharding import PartitionSpec as P


def carried_in(part, axis, combine, identity):
    place = lax.axis_index(axis)
    gathered = jax.tree.map(lambda a: lax.all_gather(a, axis), part)
    state = jax.tree.map(lambda a, e: jnp.zeros_like(a) + jnp.asarray(e, a.dtype), part, identity)

    def one(lap, state):
        return combine(
            state, jax.tree.map(lambda a: lax.dynamic_index_in_dim(a, lap, 0, False), gathered)
        )

    return lax.fori_loop(0, place, one, state)


def rotate(vectors, token_position):
    half_dim = vectors.shape[-1] // 2
    inverse = 10000.0 ** (-jnp.arange(half_dim, dtype=jnp.float32) / half_dim)
    angles = token_position.astype(jnp.float32)[:, None] * inverse[None, :]
    cosine = jnp.cos(angles)[:, None, :]
    sine_part = jnp.sin(angles)[:, None, :]
    leading = vectors[..., :half_dim]
    trailing = vectors[..., half_dim:]
    return jnp.concatenate(
        [leading * cosine - trailing * sine_part, trailing * cosine + leading * sine_part], axis=-1
    )


def chain_combine(earlier, later_part):
    return (earlier[0] * later_part[0], later_part[0][:, None, None] * earlier[1] + later_part[1])


def body(
    hidden_in,
    queries,
    keys,
    values,
    log_decay,
    retention_gain,
    norm_gain,
    routes,
    route_weights,
    w_gate,
    w_up,
    w_down,
):
    tok_rows = hidden_in.shape[1]
    model_width = hidden_in.shape[2]
    head_count = log_decay.shape[2]
    head_dim = model_width // head_count
    block_index = lax.axis_index("ctx") * lax.axis_size("exp") + lax.axis_index("exp")
    token_position = block_index * tok_rows + jnp.arange(tok_rows, dtype=jnp.int32)
    per_head_queries = (
        rotate(
            queries[0].astype(jnp.float32).reshape(tok_rows, head_count, head_dim), token_position
        )
        * head_dim ** (-0.5)
    ).astype(jnp.bfloat16)
    per_head_keys = rotate(
        keys[0].astype(jnp.float32).reshape(tok_rows, head_count, head_dim), token_position
    ).astype(jnp.bfloat16)
    per_head_values = values[0].reshape(tok_rows, head_count, head_dim)
    running_total = jnp.cumsum(log_decay[0], axis=0)
    scores = jnp.einsum(
        "thd,shd->hts", per_head_queries, per_head_keys, preferred_element_type=jnp.float32
    )
    causal = jnp.arange(tok_rows)[:, None] >= jnp.arange(tok_rows)[None, :]
    spread = running_total.T[:, :, None] - running_total.T[:, None, :]
    weights = jnp.where(
        causal[None], scores * jnp.exp(jnp.where(causal[None], spread, 0.0)), 0.0
    ).astype(jnp.bfloat16)
    inside = jnp.einsum(
        "hts,shd->thd", weights, per_head_values, preferred_element_type=jnp.float32
    )
    trailing_decay = jnp.exp(running_total[-1][None, :] - running_total)
    block_summary = jnp.einsum(
        "qpf,qpy->pfy",
        per_head_keys.astype(jnp.float32) * trailing_decay[:, :, None],
        per_head_values.astype(jnp.float32),
        precision=lax.Precision.HIGHEST,
    )
    group_logs, group_sums = (
        lax.all_gather(running_total[-1][None], "exp", axis=0, tiled=True),
        lax.all_gather(block_summary[None], "exp", axis=0, tiled=True),
    )
    group_size = lax.axis_size("exp")
    own_member = lax.axis_index("exp")
    inclusive = jnp.cumsum(group_logs, axis=0)
    exclusive = inclusive - group_logs
    entering_log = lax.dynamic_index_in_dim(exclusive, own_member, 0, keepdims=False)
    before_me = jnp.arange(group_size, dtype=jnp.int32)[:, None] < own_member
    inner_coeff = jnp.where(
        before_me, jnp.exp(jnp.where(before_me, entering_log[None, :] - inclusive, 0.0)), 0.0
    )
    inner_state = jnp.einsum(
        "jh,jhab->hab", inner_coeff, group_sums, precision=lax.Precision.HIGHEST
    )
    total_coeff = jnp.exp(inclusive[-1][None, :] - inclusive)
    group_state = jnp.einsum(
        "jh,jhab->hab", total_coeff, group_sums, precision=lax.Precision.HIGHEST
    )
    group_decay = jnp.exp(inclusive[-1])
    identity = (
        jnp.ones((head_count,), jnp.float32),
        jnp.zeros((head_count, head_dim, head_dim), jnp.float32),
    )
    leading_sum = carried_in((group_decay, group_state), "ctx", chain_combine, identity)
    state_in = jnp.exp(entering_log)[:, None, None] * leading_sum[1] + inner_state
    external_part = jnp.exp(running_total)[:, :, None] * jnp.einsum(
        "wjc,jco->wjo",
        per_head_queries.astype(jnp.float32),
        state_in,
        precision=lax.Precision.HIGHEST,
    )
    retrieved = inside + external_part
    centre = jnp.mean(retrieved, axis=-1, keepdims=True)
    deviation = retrieved - centre
    variance = jnp.mean(deviation * deviation, axis=-1, keepdims=True)
    normalized = (deviation * lax.rsqrt(variance + 1e-05)).reshape(tok_rows, model_width)
    residual = hidden_in[0].astype(jnp.float32) + retention_gain * normalized
    square_mean = jnp.mean(residual * residual, axis=-1, keepdims=True)
    normed = (residual * lax.rsqrt(square_mean + 1e-06) * norm_gain).astype(jnp.bfloat16)
    expert_count = lax.axis_size("ctx") * lax.axis_size("dp")
    top_count = routes.shape[2]
    capacity = (tok_rows * top_count * 5 + 4 * expert_count - 1) // (4 * expert_count)
    slot_count = expert_count * capacity
    route_rows = routes[0]
    expert_hits = (
        route_rows.reshape(tok_rows * top_count)[:, None]
        == jnp.arange(expert_count, dtype=jnp.int32)[None, :]
    ).astype(jnp.int32)
    earlier = jnp.cumsum(expert_hits, axis=0) - expert_hits
    slot_rank = jnp.sum(earlier * expert_hits, axis=1).reshape(tok_rows, top_count)
    destination = route_rows * capacity + slot_rank
    slot_lanes = jnp.arange(slot_count, dtype=jnp.int32)
    placing = jnp.any(destination[None, :, :] == slot_lanes[:, None, None], axis=2).astype(
        jnp.bfloat16
    )
    outgoing = jnp.dot(placing, normed, preferred_element_type=jnp.float32).astype(jnp.bfloat16)
    arrived = lax.all_to_all(
        outgoing.reshape(expert_count, capacity, model_width),
        ("ctx", "dp"),
        split_axis=0,
        concat_axis=0,
        tiled=True,
    ).reshape(slot_count, model_width)
    gate_next = jnp.dot(
        arrived,
        lax.all_gather(w_gate, "exp", axis=1, tiled=True)[0],
        preferred_element_type=jnp.float32,
    )
    up_next = jnp.dot(
        arrived,
        lax.all_gather(w_up, "exp", axis=1, tiled=True)[0],
        preferred_element_type=jnp.float32,
    )
    hidden = (jax.nn.silu(gate_next) * up_next).astype(jnp.bfloat16)
    expert_out = lax.dot_general(
        hidden,
        lax.all_gather(w_down, "exp", axis=1, tiled=True)[0],
        (((1,), (1,)), ((), ())),
        preferred_element_type=jnp.float32,
    ).astype(jnp.bfloat16)
    returned = lax.all_to_all(
        expert_out.reshape(expert_count, capacity, model_width),
        ("ctx", "dp"),
        split_axis=0,
        concat_axis=0,
        tiled=True,
    ).reshape(slot_count, model_width)
    output = residual
    for route_index in range(top_count):
        picking = (destination[:, route_index][:, None] == slot_lanes[None, :]).astype(jnp.bfloat16)
        routed = jnp.dot(picking, returned, preferred_element_type=jnp.float32)
        output = output + route_weights[0][:, route_index][:, None] * routed
    return output.astype(jnp.bfloat16)[None]


MESH = pl.DeviceIdType.MESH
BF16 = jnp.bfloat16
F32 = jnp.float32
TILE = 16


def iota(shape, dim):
    return lax.broadcasted_iota(jnp.int32, shape, dim)


def dot(a, b, contract=((1,), (0,)), precision=None):
    return lax.dot_general(
        a, b, (contract, ((), ())), precision=precision, preferred_element_type=F32
    )


def fused_kernel(
    geo,
    hid_in,
    q_in,
    k_in,
    v_in,
    ld_in,
    rgain_in,
    ngain_in,
    routes_in,
    rweights_in,
    wg,
    wu,
    wd,
    out,
    hid,
    q,
    k,
    v,
    ld,
    rgain,
    ngain,
    routes,
    rweights,
    wgb,
    wub,
    wdb,
    sum_send,
    sum_recv,
    dec_send,
    dec_recv,
    ent_send,
    ent_recv,
    disp,
    xin,
    xall,
    hidden,
    orem,
    eo,
    ret,
    qrot,
    krot,
    resid,
    in_sem,
    w_local,
    w_swap_send,
    w_swap_recv,
    w_sib_send,
    w_sib_recv,
    x_send,
    x_recv,
):
    ctx_n, exp_n, cap = geo
    nb = ctx_n * exp_n
    rows, width = hid.shape
    heads = ld.shape[0]
    hd = width // heads
    ff = wg.shape[1]
    half = wg.shape[0]
    rem_n = cap - TILE
    fold = TILE // rem_n
    fw = width // fold
    rp = width // nb
    x = lax.axis_index("exp")
    c = lax.axis_index("dp")
    me = lax.axis_index("ctx") * exp_n + x
    stays = c == x
    moves = c != x

    def peer(index):
        return {"ctx": index // exp_n, "exp": index % exp_n}

    sibling = {"dp": 1 - c}
    partner = {"exp": c, "dp": x}

    arguments = [
        pltpu.make_async_copy(src, dst, in_sem.at[i])
        for i, (src, dst) in enumerate(
            (
                (ld_in, ld),
                (k_in, k),
                (v_in, v),
                (q_in, q),
                (routes_in, routes),
                (hid_in, hid),
                (rgain_in, rgain),
                (ngain_in, ngain),
                (rweights_in, rweights),
            )
        )
    ]
    for argument in arguments:
        argument.start()

    barrier = pltpu.get_barrier_semaphore()

    def greet(d, carry):
        pl.semaphore_signal(
            barrier, inc=1, device_id=peer(lax.rem(me + d, nb)), device_id_type=MESH
        )
        return carry

    lax.fori_loop(1, nb, greet, 0)
    pl.semaphore_signal(barrier, inc=1, device_id=sibling, device_id_type=MESH)

    @pl.when(moves)
    def _():
        pl.semaphore_signal(barrier, inc=1, device_id=partner, device_id_type=MESH)

    lane = iota((rows, hd), 1)
    pair = jnp.where(lane < hd // 2, lane, lane - hd // 2).astype(F32)
    position = (me * rows + iota((rows, hd), 0)).astype(F32)
    angle = position * jnp.exp(pair * (-math.log(10000.0) / (hd // 2)))
    cosine = jnp.cos(angle)
    sine = jnp.where(lane < hd // 2, -1.0, 1.0) * jnp.sin(angle)

    @pl.when(moves)
    def _():
        pl.semaphore_wait(barrier, nb + 1)

    @pl.when(stays)
    def _():
        pl.semaphore_wait(barrier, nb)

    chunks = []
    for array, (src, buf) in enumerate(((wg, wgb), (wu, wub), (wd, wdb))):
        pieces = 4 if array == 2 else 2
        step = half // pieces
        for piece in range(pieces):
            chunks.append((src, buf, piece * step, step, array))

    def place(buf, owner, start, step):
        return buf.at[pl.ds(pl.multiple_of(owner * half + start, TILE), step)]

    def swap_copy(i):
        src, buf, start, step, _ = chunks[i]
        return pltpu.make_async_remote_copy(
            src_ref=src.at[pl.ds(start, step)],
            dst_ref=place(buf, x, start, step),
            send_sem=w_swap_send.at[i],
            recv_sem=w_swap_recv.at[i],
            device_id=partner,
            device_id_type=MESH,
        )

    def swap_arrival(i):
        src, buf, start, step, _ = chunks[i]
        return pltpu.make_async_remote_copy(
            src_ref=src.at[pl.ds(start, step)],
            dst_ref=place(buf, c, start, step),
            send_sem=w_swap_send.at[i],
            recv_sem=w_swap_recv.at[i],
            device_id=partner,
            device_id_type=MESH,
        )

    def sib_copy(i, own):
        src, buf, start, step, _ = chunks[i]
        mine = place(buf, c, start, step)
        return pltpu.make_async_remote_copy(
            src_ref=src.at[pl.ds(start, step)] if own else mine,
            dst_ref=mine,
            send_sem=w_sib_send.at[i],
            recv_sem=w_sib_recv.at[i],
            device_id=sibling,
            device_id_type=MESH,
        )

    def sib_arrival(i):
        src, buf, start, step, _ = chunks[i]
        return pltpu.make_async_remote_copy(
            src_ref=src.at[pl.ds(start, step)],
            dst_ref=place(buf, 1 - c, start, step),
            send_sem=w_sib_send.at[i],
            recv_sem=w_sib_recv.at[i],
            device_id=sibling,
            device_id_type=MESH,
        )

    def local_copy(i):
        src, buf, start, step, _ = chunks[i]
        return pltpu.make_async_copy(
            src.at[pl.ds(start, step)], place(buf, c, start, step), w_local.at[i]
        )

    def begin(first, last):
        @pl.when(moves)
        def _():
            for i in range(first, last):
                swap_copy(i).start()

        @pl.when(stays)
        def _():
            for i in range(first, last):
                sib_copy(i, True).start()
                local_copy(i).start()

    begin(0, 2)

    def chosen(array, group):
        found = [i for i in range(len(chunks)) if chunks[i][4] == array]
        if group is None:
            return found
        share = len(found) // 2
        return found[group * share : (group + 1) * share]

    def hand_on(array, group=None):
        @pl.when(moves)
        def _():
            for i in chosen(array, group):
                swap_arrival(i).wait_recv()
                sib_copy(i, False).start()

    def take(array, group=None):
        @pl.when(stays)
        def _():
            for i in chosen(array, group):
                local_copy(i).wait()

        for i in chosen(array, group):
            sib_arrival(i).wait_recv()

    def exchange(kind, src, dst, n):
        def at(ref, index):
            return ref.at[pl.ds(pl.multiple_of(index * n, n), n)]

        def copy(d, landing):
            dest = lax.rem(me + d, nb)
            return pltpu.make_async_remote_copy(
                src_ref=at(src, dest),
                dst_ref=at(dst, landing),
                send_sem=x_send.at[kind, d],
                recv_sem=x_recv.at[kind, d],
                device_id=peer(dest),
                device_id_type=MESH,
            )

        def start():
            def one(d, carry):
                copy(d, me).start()
                return carry

            lax.fori_loop(1, nb, one, 0)

        def arrive():
            def one(d, carry):
                copy(d, lax.rem(me + nb - d, nb)).wait_recv()
                return carry

            lax.fori_loop(1, nb, one, 0)

        def sent():
            def one(d, carry):
                copy(d, me).wait_send()
                return carry

            lax.fori_loop(1, nb, one, 0)

        own = pl.ds(pl.multiple_of(me * n, n), n)
        return start, arrive, sent, own, copy

    causal = iota((rows, rows), 0) >= iota((rows, rows), 1)
    upper = (iota((rows, rows), 0) <= iota((rows, rows), 1)).astype(F32)
    for argument in arguments[:4]:
        argument.wait()
    total_t = dot(ld[...], upper, precision=lax.Precision.HIGHEST)
    total = total_t.T
    last_t = total_t[:, rows - 1 : rows]
    dec_send[...] = jnp.broadcast_to(jnp.exp(last_t), dec_send.shape)
    _, arrive_s, sent_s, own_s, slice_copy = exchange(0, sum_send, sum_recv, rp)

    def dec_copy(d, landing):
        dest = lax.rem(me + d, nb)
        return pltpu.make_async_remote_copy(
            src_ref=dec_send,
            dst_ref=dec_recv.at[landing],
            send_sem=x_send.at[1, d],
            recv_sem=x_recv.at[1, d],
            device_id=peer(dest),
            device_id_type=MESH,
        )

    def dec_start(d, carry):
        dec_copy(d, me).start()
        return carry

    def dec_arrive(d, carry):
        dec_copy(d, lax.rem(me + nb - d, nb)).wait_recv()
        return carry

    def dec_sent(d, carry):
        dec_copy(d, me).wait_send()
        return carry

    lax.fori_loop(1, nb, dec_start, 0)
    for h in range(heads):
        cols = slice(h * hd, (h + 1) * hd)
        q_h = q[:, cols].astype(F32)
        k_h = k[:, cols].astype(F32)
        q_h = (q_h * cosine + pltpu.roll(q_h, hd // 2, 1) * sine) * hd ** (-0.5)
        k_h = (k_h * cosine + pltpu.roll(k_h, hd // 2, 1) * sine).astype(BF16)
        qrot[:, cols] = q_h.astype(BF16)
        krot[:, cols] = k_h
        column = total[:, h : h + 1]
        scaled = k_h.astype(F32) * jnp.exp(total[rows - 1 : rows, h : h + 1] - column)
        scaled = scaled.T
        coarse = scaled.astype(BF16)
        fine = (scaled - coarse.astype(F32)).astype(BF16)
        v_h = v[:, cols]
        sum_send[cols, :] = (dot(coarse, v_h) + dot(fine, v_h)).astype(BF16)
        for dest in range(h * hd // rp, (h + 1) * hd // rp):

            @pl.when(me != dest)
            def _():
                slice_copy(lax.rem(dest + nb - me, nb), me).start()


    begin(2, 4)
    sum_recv[own_s, :] = sum_send[own_s, :]
    dec_recv[me] = dec_send[...]

    for h in range(heads):
        cols = slice(h * hd, (h + 1) * hd)
        spread = total[:, h : h + 1] - total_t[h : h + 1, :]
        scores = dot(qrot[:, cols], krot[:, cols], ((1,), (1,)))
        weights = jnp.where(causal, scores * jnp.exp(jnp.where(causal, spread, 0.0)), 0.0)
        resid[:, cols] = dot(weights.astype(BF16), v[:, cols])

    lax.fori_loop(1, nb, dec_arrive, 0)
    arrive_s()
    head = (me * rp) // hd
    state = jnp.zeros((rp, hd), F32)
    for b in range(nb):
        part = slice(b * rp, (b + 1) * rp)
        ent_send[part, :] = state.astype(BF16)
        if b < nb - 1:
            state = dec_recv[b, pl.ds(head, 1), :] * state + sum_recv[part, :].astype(F32)
    start_e, arrive_e, sent_e, own_e, _ = exchange(2, ent_send, ent_recv, rp)
    start_e()
    for argument in arguments[4:]:
        argument.wait()
    ent_recv[own_e, :] = ent_send[own_e, :]

    by_position = jnp.concatenate(
        [routes[...].astype(F32), rweights[...], jnp.zeros((4, rows), F32)], axis=0
    ).T
    r0 = by_position[:, 0:1]
    r1 = by_position[:, 1:2]
    lanes = iota((rows, 128), 1).astype(F32)
    hits = ((r0 == lanes) | (r1 == lanes)).astype(BF16)
    strict = (iota((rows, rows), 0) > iota((rows, rows), 1)).astype(BF16)
    before = dot(strict, hits)
    slots = iota((rows, nb * TILE), 1).astype(F32)
    pick_main, pick_rem = [], []
    for r in (r0, r1):
        rank = jnp.sum(jnp.where(r == lanes, before, 0.0), axis=1, keepdims=True)
        base = r * TILE + rank
        in_main = jnp.where(rank < TILE, base, -1.0)
        in_rem = jnp.where(rank < TILE, -1.0e6, base - TILE)
        pick_main.append((in_main == slots).astype(F32))
        pick_rem.append([(in_rem + f * rem_n == slots).astype(F32) for f in range(fold)])
    put_main = (pick_main[0] + pick_main[1]).T.astype(BF16)
    put_rem = [(pick_rem[0][f] + pick_rem[1][f]).T.astype(BF16) for f in range(fold)]
    pick_main = [p.astype(BF16) for p in pick_main]
    pick_rem = [[p.astype(BF16) for p in ps] for ps in pick_rem]

    arrive_e()
    square = jnp.zeros((rows, 1), F32)
    for h in range(heads):
        cols = slice(h * hd, (h + 1) * hd)
        carried = dot(qrot[:, cols], ent_recv[cols, :])
        got = resid[:, cols] + jnp.exp(total[:, h : h + 1]) * carried
        got = got - jnp.mean(got, axis=1, keepdims=True)
        variance = jnp.mean(got * got, axis=1, keepdims=True)
        got = got * lax.rsqrt(variance + 1e-05)
        got = hid[:, cols].astype(F32) + rgain[:, cols] * got
        resid[:, cols] = got
        square = square + jnp.sum(got * got, axis=1, keepdims=True)
    normed = (resid[...] * lax.rsqrt(square / width + 1e-06) * ngain[...]).astype(BF16)

    disp[:, :width] = dot(put_main, normed).astype(BF16)
    folded = jnp.zeros((nb * TILE, fw), F32)
    for f in range(fold):
        folded = folded + dot(put_rem[f], normed[:, f * fw : (f + 1) * fw])
    disp[:, width:] = folded.astype(BF16)
    start_m, arrive_m, sent_m, own_m, _ = exchange(3, disp, xin, TILE)
    start_m()
    begin(4, 8)
    xin[own_m, :] = disp[own_m, :]

    hand_on(0)
    hand_on(1)
    arrive_m()
    xall[: nb * TILE, :] = xin[:, :width]
    row = iota((nb * rem_n, nb * TILE), 0)
    spot = (row // rem_n) * TILE + lax.rem(row, rem_n)
    for f in range(fold):
        unfold = (iota((nb * rem_n, nb * TILE), 1) == spot + f * rem_n).astype(F32)
        xall[nb * TILE :, f * fw : (f + 1) * fw] = dot(unfold.astype(BF16), xin[:, width:]).astype(
            BF16
        )

    take(0)
    take(1)

    def gate_up(i, carry):
        cols = pl.ds(pl.multiple_of(i * 128, 128), 128)
        both = dot(xall[...], jnp.concatenate([wgb[:, cols], wub[:, cols]], axis=1))
        gate = both[:, :128]
        hidden[:, cols] = (gate / (1.0 + jnp.exp(-gate)) * both[:, 128:]).astype(BF16)
        return carry

    lax.fori_loop(0, ff // 128, gate_up, 0)
    groups = 2
    part_w = half // groups
    gw = 2 * part_w
    pw = fw // groups
    column = iota((nb * TILE, nb * rem_n), 1)
    spot = (column // rem_n) * TILE + lax.rem(column, rem_n)
    returns = []
    for g in range(groups):
        hand_on(2, g)
        take(2, g)

        def down(i, carry):
            src = pl.ds(pl.multiple_of(i * half + g * part_w, part_w), part_w)
            cols = pl.ds(pl.multiple_of(i * part_w, part_w), part_w)
            result = dot(hidden[...], wdb[src, :], ((1,), (1,))).astype(BF16)
            eo[g, :, cols] = result[: nb * TILE]
            orem[:, cols] = result[nb * TILE :]
            return carry

        lax.fori_loop(0, 2, down, 0)
        folded = jnp.zeros((nb * TILE, pw), F32)
        for f in range(fold):
            refold = (iota((nb * TILE, nb * rem_n), 0) == spot + f * rem_n).astype(F32)
            folded = folded + dot(refold.astype(BF16), orem[:, f * pw : (f + 1) * pw])
        eo[g, :, gw:] = folded.astype(BF16)
        start_b, arrive_b, sent_b, own_b, _ = exchange(4 + g, eo.at[g], ret.at[g], TILE)
        start_b()
        ret[g, own_b, :] = eo[g, own_b, :]
        returns.append((arrive_b, sent_b))

    @pl.when(moves)
    def _():
        for i in range(len(chunks)):
            swap_copy(i).wait_send()
            sib_copy(i, False).wait_send()

    @pl.when(stays)
    def _():
        for i in range(len(chunks)):
            sib_copy(i, True).wait_send()

    lax.fori_loop(1, nb, dec_sent, 0)
    sent_s()
    sent_e()
    sent_m()

    for g in range(groups):
        arrive_b, sent_b = returns[g]
        arrive_b()
        for f in range(fold):
            start = f * pw
            into = (start // part_w) * half + g * part_w + start % part_w
            cols = slice(into, into + pw)
            acc = resid[:, cols]
            for j in range(2):
                routed = dot(pick_main[j], ret[g, :, start : start + pw])
                routed = routed + dot(pick_rem[j][f], ret[g, :, gw:])
                acc = acc + by_position[:, 2 + j : 3 + j] * routed
            out[:, cols] = acc.astype(BF16)
    for arrive_b, sent_b in returns:
        sent_b()


def fused(geo, *args):
    (
        hidden_in,
        queries,
        keys,
        values,
        log_decay,
        retention_gain,
        norm_gain,
        routes,
        route_weights,
        w_gate,
        w_up,
        w_down,
    ) = args
    ctx_n, exp_n, cap = geo
    nb = ctx_n * exp_n
    rows, width = hidden_in.shape[1:]
    heads = log_decay.shape[2]
    hd = width // heads
    ff = w_gate.shape[2]
    rem_n = cap - TILE
    fw = width * rem_n // TILE
    rp = width // nb
    vmem = pl.BlockSpec(memory_space=pltpu.VMEM)
    hbm = pl.BlockSpec(memory_space=pl.ANY)
    n_chunks = 8
    dma = pltpu.SemaphoreType.DMA
    out = pl.pallas_call(
        functools.partial(fused_kernel, geo),
        out_shape=jax.ShapeDtypeStruct((rows, width), BF16),
        in_specs=[hbm] * 12,
        out_specs=vmem,
        scratch_shapes=[
            pltpu.VMEM((rows, width), BF16),
            pltpu.VMEM((rows, width), BF16),
            pltpu.VMEM((rows, width), BF16),
            pltpu.VMEM((rows, width), BF16),
            pltpu.VMEM((heads, rows), F32),
            pltpu.VMEM((1, width), F32),
            pltpu.VMEM((1, width), F32),
            pltpu.VMEM((2, rows), jnp.int32),
            pltpu.VMEM((2, rows), F32),
            pltpu.VMEM((width, ff), BF16),
            pltpu.VMEM((width, ff), BF16),
            pltpu.VMEM((width, ff), BF16),
            pltpu.VMEM((width, hd), BF16),
            pltpu.VMEM((width, hd), BF16),
            pltpu.VMEM((heads, hd), F32),
            pltpu.VMEM((nb, heads, hd), F32),
            pltpu.VMEM((width, hd), BF16),
            pltpu.VMEM((width, hd), BF16),
            pltpu.VMEM((nb * TILE, width + fw), BF16),
            pltpu.VMEM((nb * TILE, width + fw), BF16),
            pltpu.VMEM((nb * cap, width), BF16),
            pltpu.VMEM((nb * cap, ff), BF16),
            pltpu.VMEM((nb * rem_n, width // 2), BF16),
            pltpu.VMEM((2, nb * TILE, (width + fw) // 2), BF16),
            pltpu.VMEM((2, nb * TILE, (width + fw) // 2), BF16),
            pltpu.VMEM((rows, width), BF16),
            pltpu.VMEM((rows, width), BF16),
            pltpu.VMEM((rows, width), F32),
            dma((9,)),
            dma((n_chunks,)),
            dma((n_chunks,)),
            dma((n_chunks,)),
            dma((n_chunks,)),
            dma((n_chunks,)),
            dma((6, nb)),
            dma((6, nb)),
        ],
        compiler_params=pltpu.CompilerParams(
            collective_id=0, has_side_effects=True, vmem_limit_bytes=63 * 1024 * 1024
        ),
    )(
        hidden_in[0],
        queries[0],
        keys[0],
        values[0],
        log_decay[0].T,
        retention_gain[None],
        norm_gain[None],
        routes[0].T,
        route_weights[0].T,
        w_gate[0],
        w_up[0],
        w_down[0],
    )
    return out[None]


def geometry(args):
    ctx_n, exp_n, dp_n = (lax.axis_size(a) for a in ("ctx", "exp", "dp"))
    nb = ctx_n * exp_n
    rows, width = args[0].shape[1:]
    heads = args[4].shape[2]
    hd = width // heads
    top = args[7].shape[2]
    experts = ctx_n * dp_n
    cap = (rows * top * 5 + 4 * experts - 1) // (4 * experts)
    rem_n = cap - TILE
    fits = (
        exp_n == 2
        and dp_n == 2
        and top == 2
        and experts <= 128
        and 0 < rem_n < TILE
        and TILE % rem_n == 0
        and (width * rem_n) % (TILE * 256) == 0
        and rem_n * 2 <= TILE
        and nb * rem_n % TILE == 0
        and hd == 128
        and rows == 128
        and heads == 8
        and width % nb == 0
        and (width // nb) % TILE == 0
        and hd % (width // nb) == 0
        and args[9].shape[2] % 128 == 0
        and width % 256 == 0
        and args[9].shape[1] * 2 == width
    )
    return (ctx_n, exp_n, cap) if fits else None


def layer(*args):
    geo = geometry(args)
    return body(*args) if geo is None else fused(geo, *args)


def solution(mesh):
    in_specs = (
        P("dp", ("ctx", "exp"), None),
        P("dp", ("ctx", "exp"), None),
        P("dp", ("ctx", "exp"), None),
        P("dp", ("ctx", "exp"), None),
        P("dp", ("ctx", "exp"), None),
        P(),
        P(),
        P("dp", ("ctx", "exp"), None),
        P("dp", ("ctx", "exp"), None),
        P(("ctx", "dp"), "exp", None),
        P(("ctx", "dp"), "exp", None),
        P(("ctx", "dp"), "exp", None),
    )
    out_specs = P("dp", ("ctx", "exp"), None)
    return jax.shard_map(layer, mesh=mesh, in_specs=in_specs, out_specs=out_specs, check_vma=False)
```

```python
import functools
import math

import jax
import jax.numpy as jnp
from jax import lax
from jax.experimental import pallas as pl
from jax.experimental.pallas import tpu as pltpu
from jax.sharding import PartitionSpec as P


def carried_in(part, axis, combine, identity):
    place = lax.axis_index(axis)
    gathered = jax.tree.map(lambda a: lax.all_gather(a, axis), part)
    state = jax.tree.map(lambda a, e: jnp.zeros_like(a) + jnp.asarray(e, a.dtype), part, identity)

    def one(lap, state):
        return combine(
            state, jax.tree.map(lambda a: lax.dynamic_index_in_dim(a, lap, 0, False), gathered)
        )

    return lax.fori_loop(0, place, one, state)


def rotate(vectors, token_position):
    half_dim = vectors.shape[-1] // 2
    inverse = 10000.0 ** (-jnp.arange(half_dim, dtype=jnp.float32) / half_dim)
    angles = token_position.astype(jnp.float32)[:, None] * inverse[None, :]
    cosine = jnp.cos(angles)[:, None, :]
    sine_part = jnp.sin(angles)[:, None, :]
    leading = vectors[..., :half_dim]
    trailing = vectors[..., half_dim:]
    return jnp.concatenate(
        [leading * cosine - trailing * sine_part, trailing * cosine + leading * sine_part], axis=-1
    )


def chain_combine(earlier, later_part):
    return (earlier[0] * later_part[0], later_part[0][:, None, None] * earlier[1] + later_part[1])


def body(
    hidden_in,
    queries,
    keys,
    values,
    log_decay,
    retention_gain,
    norm_gain,
    routes,
    route_weights,
    w_gate,
    w_up,
    w_down,
):
    tok_rows = hidden_in.shape[1]
    model_width = hidden_in.shape[2]
    head_count = log_decay.shape[2]
    head_dim = model_width // head_count
    block_index = lax.axis_index("ctx") * lax.axis_size("exp") + lax.axis_index("exp")
    token_position = block_index * tok_rows + jnp.arange(tok_rows, dtype=jnp.int32)
    per_head_queries = (
        rotate(
            queries[0].astype(jnp.float32).reshape(tok_rows, head_count, head_dim), token_position
        )
        * head_dim ** (-0.5)
    ).astype(jnp.bfloat16)
    per_head_keys = rotate(
        keys[0].astype(jnp.float32).reshape(tok_rows, head_count, head_dim), token_position
    ).astype(jnp.bfloat16)
    per_head_values = values[0].reshape(tok_rows, head_count, head_dim)
    running_total = jnp.cumsum(log_decay[0], axis=0)
    scores = jnp.einsum(
        "thd,shd->hts", per_head_queries, per_head_keys, preferred_element_type=jnp.float32
    )
    causal = jnp.arange(tok_rows)[:, None] >= jnp.arange(tok_rows)[None, :]
    spread = running_total.T[:, :, None] - running_total.T[:, None, :]
    weights = jnp.where(
        causal[None], scores * jnp.exp(jnp.where(causal[None], spread, 0.0)), 0.0
    ).astype(jnp.bfloat16)
    inside = jnp.einsum(
        "hts,shd->thd", weights, per_head_values, preferred_element_type=jnp.float32
    )
    trailing_decay = jnp.exp(running_total[-1][None, :] - running_total)
    block_summary = jnp.einsum(
        "qpf,qpy->pfy",
        per_head_keys.astype(jnp.float32) * trailing_decay[:, :, None],
        per_head_values.astype(jnp.float32),
        precision=lax.Precision.HIGHEST,
    )
    group_logs, group_sums = (
        lax.all_gather(running_total[-1][None], "exp", axis=0, tiled=True),
        lax.all_gather(block_summary[None], "exp", axis=0, tiled=True),
    )
    group_size = lax.axis_size("exp")
    own_member = lax.axis_index("exp")
    inclusive = jnp.cumsum(group_logs, axis=0)
    exclusive = inclusive - group_logs
    entering_log = lax.dynamic_index_in_dim(exclusive, own_member, 0, keepdims=False)
    before_me = jnp.arange(group_size, dtype=jnp.int32)[:, None] < own_member
    inner_coeff = jnp.where(
        before_me, jnp.exp(jnp.where(before_me, entering_log[None, :] - inclusive, 0.0)), 0.0
    )
    inner_state = jnp.einsum(
        "jh,jhab->hab", inner_coeff, group_sums, precision=lax.Precision.HIGHEST
    )
    total_coeff = jnp.exp(inclusive[-1][None, :] - inclusive)
    group_state = jnp.einsum(
        "jh,jhab->hab", total_coeff, group_sums, precision=lax.Precision.HIGHEST
    )
    group_decay = jnp.exp(inclusive[-1])
    identity = (
        jnp.ones((head_count,), jnp.float32),
        jnp.zeros((head_count, head_dim, head_dim), jnp.float32),
    )
    leading_sum = carried_in((group_decay, group_state), "ctx", chain_combine, identity)
    state_in = jnp.exp(entering_log)[:, None, None] * leading_sum[1] + inner_state
    external_part = jnp.exp(running_total)[:, :, None] * jnp.einsum(
        "wjc,jco->wjo",
        per_head_queries.astype(jnp.float32),
        state_in,
        precision=lax.Precision.HIGHEST,
    )
    retrieved = inside + external_part
    centre = jnp.mean(retrieved, axis=-1, keepdims=True)
    deviation = retrieved - centre
    variance = jnp.mean(deviation * deviation, axis=-1, keepdims=True)
    normalized = (deviation * lax.rsqrt(variance + 1e-05)).reshape(tok_rows, model_width)
    residual = hidden_in[0].astype(jnp.float32) + retention_gain * normalized
    square_mean = jnp.mean(residual * residual, axis=-1, keepdims=True)
    normed = (residual * lax.rsqrt(square_mean + 1e-06) * norm_gain).astype(jnp.bfloat16)
    expert_count = lax.axis_size("ctx") * lax.axis_size("dp")
    top_count = routes.shape[2]
    capacity = (tok_rows * top_count * 5 + 4 * expert_count - 1) // (4 * expert_count)
    slot_count = expert_count * capacity
    route_rows = routes[0]
    expert_hits = (
        route_rows.reshape(tok_rows * top_count)[:, None]
        == jnp.arange(expert_count, dtype=jnp.int32)[None, :]
    ).astype(jnp.int32)
    earlier = jnp.cumsum(expert_hits, axis=0) - expert_hits
    slot_rank = jnp.sum(earlier * expert_hits, axis=1).reshape(tok_rows, top_count)
    destination = route_rows * capacity + slot_rank
    slot_lanes = jnp.arange(slot_count, dtype=jnp.int32)
    placing = jnp.any(destination[None, :, :] == slot_lanes[:, None, None], axis=2).astype(
        jnp.bfloat16
    )
    outgoing = jnp.dot(placing, normed, preferred_element_type=jnp.float32).astype(jnp.bfloat16)
    arrived = lax.all_to_all(
        outgoing.reshape(expert_count, capacity, model_width),
        ("ctx", "dp"),
        split_axis=0,
        concat_axis=0,
        tiled=True,
    ).reshape(slot_count, model_width)
    gate_next = jnp.dot(
        arrived,
        lax.all_gather(w_gate, "exp", axis=1, tiled=True)[0],
        preferred_element_type=jnp.float32,
    )
    up_next = jnp.dot(
        arrived,
        lax.all_gather(w_up, "exp", axis=1, tiled=True)[0],
        preferred_element_type=jnp.float32,
    )
    hidden = (jax.nn.silu(gate_next) * up_next).astype(jnp.bfloat16)
    expert_out = lax.dot_general(
        hidden,
        lax.all_gather(w_down, "exp", axis=1, tiled=True)[0],
        (((1,), (1,)), ((), ())),
        preferred_element_type=jnp.float32,
    ).astype(jnp.bfloat16)
    returned = lax.all_to_all(
        expert_out.reshape(expert_count, capacity, model_width),
        ("ctx", "dp"),
        split_axis=0,
        concat_axis=0,
        tiled=True,
    ).reshape(slot_count, model_width)
    output = residual
    for route_index in range(top_count):
        picking = (destination[:, route_index][:, None] == slot_lanes[None, :]).astype(jnp.bfloat16)
        routed = jnp.dot(picking, returned, preferred_element_type=jnp.float32)
        output = output + route_weights[0][:, route_index][:, None] * routed
    return output.astype(jnp.bfloat16)[None]


MESH = pl.DeviceIdType.MESH
BF16 = jnp.bfloat16
F32 = jnp.float32
TILE = 16


def iota(shape, dim):
    return lax.broadcasted_iota(jnp.int32, shape, dim)


def dot(a, b, contract=((1,), (0,)), precision=None):
    return lax.dot_general(
        a, b, (contract, ((), ())), precision=precision, preferred_element_type=F32
    )


def fused_kernel(
    geo,
    hid_in,
    q_in,
    k_in,
    v_in,
    ld_in,
    rgain_in,
    ngain_in,
    routes_in,
    rweights_in,
    wg,
    wu,
    wd,
    out,
    hid,
    q,
    k,
    v,
    ld,
    rgain,
    ngain,
    routes,
    rweights,
    wgb,
    wub,
    wdb,
    sum_send,
    sum_recv,
    dec_send,
    dec_recv,
    ent_send,
    ent_recv,
    disp,
    xin,
    xall,
    hidden,
    orem,
    eo,
    ret,
    qrot,
    krot,
    resid,
    in_sem,
    w_local,
    w_swap_send,
    w_swap_recv,
    w_sib_send,
    w_sib_recv,
    x_send,
    x_recv,
):
    ctx_n, exp_n, cap = geo
    nb = ctx_n * exp_n
    rows, width = hid.shape
    heads = ld.shape[0]
    hd = width // heads
    ff = wg.shape[1]
    half = wg.shape[0]
    rem_n = cap - TILE
    fold = TILE // rem_n
    fw = width // fold
    rp = width // nb
    x = lax.axis_index("exp")
    c = lax.axis_index("dp")
    me = lax.axis_index("ctx") * exp_n + x
    stays = c == x
    moves = c != x

    def peer(index):
        return {"ctx": index // exp_n, "exp": index % exp_n}

    sibling = {"dp": 1 - c}
    partner = {"exp": c, "dp": x}

    arguments = [
        pltpu.make_async_copy(src, dst, in_sem.at[i])
        for i, (src, dst) in enumerate(
            (
                (ld_in, ld),
                (k_in, k),
                (v_in, v),
                (q_in, q),
                (routes_in, routes),
                (hid_in, hid),
                (rgain_in, rgain),
                (ngain_in, ngain),
                (rweights_in, rweights),
            )
        )
    ]
    for argument in arguments:
        argument.start()

    barrier = pltpu.get_barrier_semaphore()

    def greet(d, carry):
        pl.semaphore_signal(
            barrier, inc=1, device_id=peer(lax.rem(me + d, nb)), device_id_type=MESH
        )
        return carry

    lax.fori_loop(1, nb, greet, 0)
    pl.semaphore_signal(barrier, inc=1, device_id=sibling, device_id_type=MESH)

    @pl.when(moves)
    def _():
        pl.semaphore_signal(barrier, inc=1, device_id=partner, device_id_type=MESH)

    lane = iota((rows, hd), 1)
    pair = jnp.where(lane < hd // 2, lane, lane - hd // 2).astype(F32)
    position = (me * rows + iota((rows, hd), 0)).astype(F32)
    angle = position * jnp.exp(pair * (-math.log(10000.0) / (hd // 2)))
    cosine = jnp.cos(angle)
    sine = jnp.where(lane < hd // 2, -1.0, 1.0) * jnp.sin(angle)

    @pl.when(moves)
    def _():
        pl.semaphore_wait(barrier, nb + 1)

    @pl.when(stays)
    def _():
        pl.semaphore_wait(barrier, nb)

    chunks = []
    for array, (src, buf) in enumerate(((wg, wgb), (wu, wub), (wd, wdb))):
        pieces = 4 if array == 2 else 2
        step = half // pieces
        for piece in range(pieces):
            chunks.append((src, buf, piece * step, step, array))

    def place(buf, owner, start, step):
        return buf.at[pl.ds(pl.multiple_of(owner * half + start, TILE), step)]

    def swap_copy(i):
        src, buf, start, step, _ = chunks[i]
        return pltpu.make_async_remote_copy(
            src_ref=src.at[pl.ds(start, step)],
            dst_ref=place(buf, x, start, step),
            send_sem=w_swap_send.at[i],
            recv_sem=w_swap_recv.at[i],
            device_id=partner,
            device_id_type=MESH,
        )

    def swap_arrival(i):
        src, buf, start, step, _ = chunks[i]
        return pltpu.make_async_remote_copy(
            src_ref=src.at[pl.ds(start, step)],
            dst_ref=place(buf, c, start, step),
            send_sem=w_swap_send.at[i],
            recv_sem=w_swap_recv.at[i],
            device_id=partner,
            device_id_type=MESH,
        )

    def sib_copy(i, own):
        src, buf, start, step, _ = chunks[i]
        mine = place(buf, c, start, step)
        return pltpu.make_async_remote_copy(
            src_ref=src.at[pl.ds(start, step)] if own else mine,
            dst_ref=mine,
            send_sem=w_sib_send.at[i],
            recv_sem=w_sib_recv.at[i],
            device_id=sibling,
            device_id_type=MESH,
        )

    def sib_arrival(i):
        src, buf, start, step, _ = chunks[i]
        return pltpu.make_async_remote_copy(
            src_ref=src.at[pl.ds(start, step)],
            dst_ref=place(buf, 1 - c, start, step),
            send_sem=w_sib_send.at[i],
            recv_sem=w_sib_recv.at[i],
            device_id=sibling,
            device_id_type=MESH,
        )

    def local_copy(i):
        src, buf, start, step, _ = chunks[i]
        return pltpu.make_async_copy(
            src.at[pl.ds(start, step)], place(buf, c, start, step), w_local.at[i]
        )

    def begin(first, last):
        @pl.when(moves)
        def _():
            for i in range(first, last):
                swap_copy(i).start()

        @pl.when(stays)
        def _():
            for i in range(first, last):
                sib_copy(i, True).start()
                local_copy(i).start()

    begin(0, 2)

    def chosen(array, group):
        found = [i for i in range(len(chunks)) if chunks[i][4] == array]
        if group is None:
            return found
        share = len(found) // 2
        return found[group * share : (group + 1) * share]

    def hand_on(array, group=None):
        @pl.when(moves)
        def _():
            for i in chosen(array, group):
                swap_arrival(i).wait_recv()
                sib_copy(i, False).start()

    def take(array, group=None):
        @pl.when(stays)
        def _():
            for i in chosen(array, group):
                local_copy(i).wait()

        for i in chosen(array, group):
            sib_arrival(i).wait_recv()

    def exchange(kind, src, dst, n):
        def at(ref, index):
            return ref.at[pl.ds(pl.multiple_of(index * n, n), n)]

        def copy(d, landing):
            dest = lax.rem(me + d, nb)
            return pltpu.make_async_remote_copy(
                src_ref=at(src, dest),
                dst_ref=at(dst, landing),
                send_sem=x_send.at[kind, d],
                recv_sem=x_recv.at[kind, d],
                device_id=peer(dest),
                device_id_type=MESH,
            )

        def start():
            def one(d, carry):
                copy(d, me).start()
                return carry

            lax.fori_loop(1, nb, one, 0)

        def arrive():
            def one(d, carry):
                copy(d, lax.rem(me + nb - d, nb)).wait_recv()
                return carry

            lax.fori_loop(1, nb, one, 0)

        def sent():
            def one(d, carry):
                copy(d, me).wait_send()
                return carry

            lax.fori_loop(1, nb, one, 0)

        own = pl.ds(pl.multiple_of(me * n, n), n)
        return start, arrive, sent, own, copy

    causal = iota((rows, rows), 0) >= iota((rows, rows), 1)
    upper = (iota((rows, rows), 0) <= iota((rows, rows), 1)).astype(F32)
    for argument in arguments[:4]:
        argument.wait()
    total_t = dot(ld[...], upper, precision=lax.Precision.HIGHEST)
    total = total_t.T
    last_t = total_t[:, rows - 1 : rows]
    dec_send[...] = jnp.broadcast_to(jnp.exp(last_t), dec_send.shape)
    _, arrive_s, sent_s, own_s, slice_copy = exchange(0, sum_send, sum_recv, rp)

    def dec_copy(d, landing):
        dest = lax.rem(me + d, nb)
        return pltpu.make_async_remote_copy(
            src_ref=dec_send,
            dst_ref=dec_recv.at[landing],
            send_sem=x_send.at[1, d],
            recv_sem=x_recv.at[1, d],
            device_id=peer(dest),
            device_id_type=MESH,
        )

    def dec_start(d, carry):
        dec_copy(d, me).start()
        return carry

    def dec_arrive(d, carry):
        dec_copy(d, lax.rem(me + nb - d, nb)).wait_recv()
        return carry

    def dec_sent(d, carry):
        dec_copy(d, me).wait_send()
        return carry

    lax.fori_loop(1, nb, dec_start, 0)
    for h in range(heads):
        cols = slice(h * hd, (h + 1) * hd)
        q_h = q[:, cols].astype(F32)
        k_h = k[:, cols].astype(F32)
        q_h = (q_h * cosine + pltpu.roll(q_h, hd // 2, 1) * sine) * hd ** (-0.5)
        k_h = (k_h * cosine + pltpu.roll(k_h, hd // 2, 1) * sine).astype(BF16)
        qrot[:, cols] = q_h.astype(BF16)
        krot[:, cols] = k_h
        column = total[:, h : h + 1]
        scaled = k_h.astype(F32) * jnp.exp(total[rows - 1 : rows, h : h + 1] - column)
        scaled = scaled.T
        coarse = scaled.astype(BF16)
        fine = (scaled - coarse.astype(F32)).astype(BF16)
        v_h = v[:, cols]
        sum_send[cols, :] = (dot(coarse, v_h) + dot(fine, v_h)).astype(BF16)
        for dest in range(h * hd // rp, (h + 1) * hd // rp):

            @pl.when(me != dest)
            def _():
                slice_copy(lax.rem(dest + nb - me, nb), me).start()


    begin(2, 4)
    sum_recv[own_s, :] = sum_send[own_s, :]
    dec_recv[me] = dec_send[...]

    for h in range(heads):
        cols = slice(h * hd, (h + 1) * hd)
        spread = total[:, h : h + 1] - total_t[h : h + 1, :]
        scores = dot(qrot[:, cols], krot[:, cols], ((1,), (1,)))
        weights = jnp.where(causal, scores * jnp.exp(jnp.where(causal, spread, 0.0)), 0.0)
        resid[:, cols] = dot(weights.astype(BF16), v[:, cols])

    lax.fori_loop(1, nb, dec_arrive, 0)
    arrive_s()
    head = (me * rp) // hd
    state = jnp.zeros((rp, hd), F32)
    for b in range(nb):
        part = slice(b * rp, (b + 1) * rp)
        ent_send[part, :] = state.astype(BF16)
        if b < nb - 1:
            state = dec_recv[b, pl.ds(head, 1), :] * state + sum_recv[part, :].astype(F32)
    start_e, arrive_e, sent_e, own_e, _ = exchange(2, ent_send, ent_recv, rp)
    start_e()
    for argument in arguments[4:]:
        argument.wait()
    ent_recv[own_e, :] = ent_send[own_e, :]

    by_position = jnp.concatenate(
        [routes[...].astype(F32), rweights[...], jnp.zeros((4, rows), F32)], axis=0
    ).T
    r0 = by_position[:, 0:1]
    r1 = by_position[:, 1:2]
    lanes = iota((rows, 128), 1).astype(F32)
    hits = ((r0 == lanes) | (r1 == lanes)).astype(BF16)
    strict = (iota((rows, rows), 0) > iota((rows, rows), 1)).astype(BF16)
    before = dot(strict, hits)
    slots = iota((rows, nb * TILE), 1).astype(F32)
    pick_main, pick_rem = [], []
    for r in (r0, r1):
        rank = jnp.sum(jnp.where(r == lanes, before, 0.0), axis=1, keepdims=True)
        base = r * TILE + rank
        in_main = jnp.where(rank < TILE, base, -1.0)
        in_rem = jnp.where(rank < TILE, -1.0e6, base - TILE)
        pick_main.append((in_main == slots).astype(F32))
        pick_rem.append([(in_rem + f * rem_n == slots).astype(F32) for f in range(fold)])
    put_main = (pick_main[0] + pick_main[1]).T.astype(BF16)
    put_rem = [(pick_rem[0][f] + pick_rem[1][f]).T.astype(BF16) for f in range(fold)]
    pick_main = [p.astype(BF16) for p in pick_main]
    pick_rem = [[p.astype(BF16) for p in ps] for ps in pick_rem]

    arrive_e()
    square = jnp.zeros((rows, 1), F32)
    for h in range(heads):
        cols = slice(h * hd, (h + 1) * hd)
        carried = dot(qrot[:, cols], ent_recv[cols, :])
        got = resid[:, cols] + jnp.exp(total[:, h : h + 1]) * carried
        got = got - jnp.mean(got, axis=1, keepdims=True)
        variance = jnp.mean(got * got, axis=1, keepdims=True)
        got = got * lax.rsqrt(variance + 1e-05)
        got = hid[:, cols].astype(F32) + rgain[:, cols] * got
        resid[:, cols] = got
        square = square + jnp.sum(got * got, axis=1, keepdims=True)
    normed = (resid[...] * lax.rsqrt(square / width + 1e-06) * ngain[...]).astype(BF16)

    disp[:, :width] = dot(put_main, normed).astype(BF16)
    folded = jnp.zeros((nb * TILE, fw), F32)
    for f in range(fold):
        folded = folded + dot(put_rem[f], normed[:, f * fw : (f + 1) * fw])
    disp[:, width:] = folded.astype(BF16)
    start_m, arrive_m, sent_m, own_m, _ = exchange(3, disp, xin, TILE)
    start_m()
    begin(4, 8)
    xin[own_m, :] = disp[own_m, :]

    hand_on(0)
    hand_on(1)
    arrive_m()
    xall[: nb * TILE, :] = xin[:, :width]
    row = iota((nb * rem_n, nb * TILE), 0)
    spot = (row // rem_n) * TILE + lax.rem(row, rem_n)
    for f in range(fold):
        unfold = (iota((nb * rem_n, nb * TILE), 1) == spot + f * rem_n).astype(F32)
        xall[nb * TILE :, f * fw : (f + 1) * fw] = dot(unfold.astype(BF16), xin[:, width:]).astype(
            BF16
        )

    take(0)
    take(1)

    def gate_up(i, carry):
        cols = pl.ds(pl.multiple_of(i * 128, 128), 128)
        both = dot(xall[...], jnp.concatenate([wgb[:, cols], wub[:, cols]], axis=1))
        gate = both[:, :128]
        hidden[:, cols] = (gate / (1.0 + jnp.exp(-gate)) * both[:, 128:]).astype(BF16)
        return carry

    lax.fori_loop(0, ff // 128, gate_up, 0)
    part_w = half // 2
    hw = half + fw // 2
    pw = fw // 2
    column = iota((nb * TILE, nb * rem_n), 1)
    spot = (column // rem_n) * TILE + lax.rem(column, rem_n)

    def down(which, part):
        src = pl.ds(pl.multiple_of(which * half + part * part_w, part_w), part_w)
        cols = pl.ds(pl.multiple_of(which * hw + part * part_w, 128), part_w)
        result = dot(hidden[...], wdb[src, :], ((1,), (1,))).astype(BF16)
        eo[:, cols] = result[: nb * TILE]
        orem[:, part * part_w : (part + 1) * part_w] = result[nb * TILE :]

    def fold_rest(which):
        folded = jnp.zeros((nb * TILE, pw), F32)
        for f in range(fold):
            refold = (iota((nb * TILE, nb * rem_n), 0) == spot + f * rem_n).astype(F32)
            folded = folded + dot(refold.astype(BF16), orem[:, f * pw : (f + 1) * pw])
        eo[:, pl.ds(pl.multiple_of(which * hw + half, 128), pw)] = folded.astype(BF16)

    def give_back(kind, swapped, first, span):
        def at(ref, index, owner):
            which = 1 - owner if swapped else owner
            cols = pl.ds(pl.multiple_of(which * hw + first, 128), span)
            return ref.at[pl.ds(pl.multiple_of(index * TILE, TILE), TILE), cols]

        def copy(d, landing, owner):
            dest = lax.rem(me + d, nb)
            return pltpu.make_async_remote_copy(
                src_ref=at(eo, dest, x),
                dst_ref=at(ret, landing, owner),
                send_sem=x_send.at[kind, d],
                recv_sem=x_recv.at[kind, d],
                device_id=peer(dest),
                device_id_type=MESH,
            )

        def one(d, carry):
            copy(d, me, x).start()
            return carry

        lax.fori_loop(1, nb, one, 0)

        def arrive():
            def one(d, carry):
                source = lax.rem(me + nb - d, nb)
                copy(d, source, lax.rem(source, exp_n)).wait_recv()
                return carry

            lax.fori_loop(1, nb, one, 0)

        def sent():
            def one(d, carry):
                copy(d, me, x).wait_send()
                return carry

            lax.fori_loop(1, nb, one, 0)

        return arrive, sent

    returns = []

    @pl.when(stays)
    def _():
        for i in chosen(2, None):
            local_copy(i).wait()

    @pl.when(moves)
    def _():
        for i in chosen(2, None):
            sib_arrival(i).wait_recv()

    down(x, 0)
    down(x, 1)
    fold_rest(x)
    returns.append(give_back(4, False, 0, hw))
    for part in range(2):
        hand_on(2, part)

        @pl.when(stays)
        def _():
            for i in chosen(2, part):
                sib_arrival(i).wait_recv()

        down(1 - x, part)
        if part == 1:
            fold_rest(1 - x)
            returns.append(give_back(6, True, part_w, hw - part_w))
        else:
            returns.append(give_back(5, True, 0, part_w))
    own = pl.ds(pl.multiple_of(me * TILE, TILE), TILE)
    ret[own, :] = eo[own, :]

    @pl.when(moves)
    def _():
        for i in range(len(chunks)):
            swap_copy(i).wait_send()
            sib_copy(i, False).wait_send()

    @pl.when(stays)
    def _():
        for i in range(len(chunks)):
            sib_copy(i, True).wait_send()

    lax.fori_loop(1, nb, dec_sent, 0)
    sent_s()
    sent_e()
    sent_m()

    for arrive_b, sent_b in returns:
        arrive_b()
    for which in range(2):
        for f in range(fold):
            cols = slice(which * half + f * pw, which * half + (f + 1) * pw)
            got = slice(which * hw + f * pw, which * hw + (f + 1) * pw)
            rest = slice(which * hw + half, (which + 1) * hw)
            acc = resid[:, cols]
            for j in range(2):
                routed = dot(pick_main[j], ret[:, got]) + dot(pick_rem[j][f], ret[:, rest])
                acc = acc + by_position[:, 2 + j : 3 + j] * routed
            out[:, cols] = acc.astype(BF16)
    for arrive_b, sent_b in returns:
        sent_b()


def fused(geo, *args):
    (
        hidden_in,
        queries,
        keys,
        values,
        log_decay,
        retention_gain,
        norm_gain,
        routes,
        route_weights,
        w_gate,
        w_up,
        w_down,
    ) = args
    ctx_n, exp_n, cap = geo
    nb = ctx_n * exp_n
    rows, width = hidden_in.shape[1:]
    heads = log_decay.shape[2]
    hd = width // heads
    ff = w_gate.shape[2]
    rem_n = cap - TILE
    fw = width * rem_n // TILE
    rp = width // nb
    vmem = pl.BlockSpec(memory_space=pltpu.VMEM)
    hbm = pl.BlockSpec(memory_space=pl.ANY)
    n_chunks = 8
    dma = pltpu.SemaphoreType.DMA
    out = pl.pallas_call(
        functools.partial(fused_kernel, geo),
        out_shape=jax.ShapeDtypeStruct((rows, width), BF16),
        in_specs=[hbm] * 12,
        out_specs=vmem,
        scratch_shapes=[
            pltpu.VMEM((rows, width), BF16),
            pltpu.VMEM((rows, width), BF16),
            pltpu.VMEM((rows, width), BF16),
            pltpu.VMEM((rows, width), BF16),
            pltpu.VMEM((heads, rows), F32),
            pltpu.VMEM((1, width), F32),
            pltpu.VMEM((1, width), F32),
            pltpu.VMEM((2, rows), jnp.int32),
            pltpu.VMEM((2, rows), F32),
            pltpu.VMEM((width, ff), BF16),
            pltpu.VMEM((width, ff), BF16),
            pltpu.VMEM((width, ff), BF16),
            pltpu.VMEM((width, hd), BF16),
            pltpu.VMEM((width, hd), BF16),
            pltpu.VMEM((heads, hd), F32),
            pltpu.VMEM((nb, heads, hd), F32),
            pltpu.VMEM((width, hd), BF16),
            pltpu.VMEM((width, hd), BF16),
            pltpu.VMEM((nb * TILE, width + fw), BF16),
            pltpu.VMEM((nb * TILE, width + fw), BF16),
            pltpu.VMEM((nb * cap, width), BF16),
            pltpu.VMEM((nb * cap, ff), BF16),
            pltpu.VMEM((nb * rem_n, width // 2), BF16),
            pltpu.VMEM((nb * TILE, width + fw), BF16),
            pltpu.VMEM((nb * TILE, width + fw), BF16),
            pltpu.VMEM((rows, width), BF16),
            pltpu.VMEM((rows, width), BF16),
            pltpu.VMEM((rows, width), F32),
            dma((9,)),
            dma((n_chunks,)),
            dma((n_chunks,)),
            dma((n_chunks,)),
            dma((n_chunks,)),
            dma((n_chunks,)),
            dma((7, nb)),
            dma((7, nb)),
        ],
        compiler_params=pltpu.CompilerParams(
            collective_id=0, has_side_effects=True, vmem_limit_bytes=63 * 1024 * 1024
        ),
    )(
        hidden_in[0],
        queries[0],
        keys[0],
        values[0],
        log_decay[0].T,
        retention_gain[None],
        norm_gain[None],
        routes[0].T,
        route_weights[0].T,
        w_gate[0],
        w_up[0],
        w_down[0],
    )
    return out[None]


def geometry(args):
    ctx_n, exp_n, dp_n = (lax.axis_size(a) for a in ("ctx", "exp", "dp"))
    nb = ctx_n * exp_n
    rows, width = args[0].shape[1:]
    heads = args[4].shape[2]
    hd = width // heads
    top = args[7].shape[2]
    experts = ctx_n * dp_n
    cap = (rows * top * 5 + 4 * experts - 1) // (4 * experts)
    rem_n = cap - TILE
    fits = (
        exp_n == 2
        and dp_n == 2
        and top == 2
        and experts <= 128
        and 0 < rem_n < TILE
        and TILE % rem_n == 0
        and (width * rem_n) % (TILE * 256) == 0
        and rem_n * 2 <= TILE
        and nb * rem_n % TILE == 0
        and hd == 128
        and rows == 128
        and heads == 8
        and width % nb == 0
        and (width // nb) % TILE == 0
        and hd % (width // nb) == 0
        and args[9].shape[2] % 128 == 0
        and width % 256 == 0
        and args[9].shape[1] * 2 == width
    )
    return (ctx_n, exp_n, cap) if fits else None


def layer(*args):
    geo = geometry(args)
    return body(*args) if geo is None else fused(geo, *args)


def solution(mesh):
    in_specs = (
        P("dp", ("ctx", "exp"), None),
        P("dp", ("ctx", "exp"), None),
        P("dp", ("ctx", "exp"), None),
        P("dp", ("ctx", "exp"), None),
        P("dp", ("ctx", "exp"), None),
        P(),
        P(),
        P("dp", ("ctx", "exp"), None),
        P("dp", ("ctx", "exp"), None),
        P(("ctx", "dp"), "exp", None),
        P(("ctx", "dp"), "exp", None),
        P(("ctx", "dp"), "exp", None),
    )
    out_specs = P("dp", ("ctx", "exp"), None)
    return jax.shard_map(layer, mesh=mesh, in_specs=in_specs, out_specs=out_specs, check_vma=False)
```
